256 devices in a mesh: wide: 16 (over x, z_lo), narrow: 16 (over z_hi, y, core).
Axes of the slice: x: 4, y: 4, z: 8 (z_hi: 2, z_lo: 4; z = z_hi * 4 + z_lo), core: 2. Of those that a mesh axis runs over, the one named last changes fastest.
Arguments:
- basis: float32 [65536, 8192], P('wide', 'narrow'), may hold values from -0.0234375 to 0.0234375
- conf_values: float32 [8192], P('narrow'), may hold values from 0.5 to 8
- task_basis: float32 [128, 128], replicated, may hold values from -0.5 to 0.5
- task_values: float32 [128], replicated, may hold values from 0.5 to 4
- noise: float32 [1], replicated, may hold values from 0.2 to 1
- observations: float32 [65536, 128], P(('wide', 'narrow')), may hold values from -6 to 6
- train_codes: int32 [65536], P(('wide', 'narrow')), may hold values from 0 to 1048575
- length_scales: float32 [10], replicated, may hold values from 0.03 to 0.3
- signal: float32 [1], replicated, may hold values from 0.03 to 0.1
- cand_codes: int32 [32768], P('wide'), may hold values from 0 to 1048575
Outputs:
- coefficients: float32 [65536, 128], P(('wide', 'narrow'))
- means: float32 [32768, 128], P(('wide', 'narrow'))
The draws below stay inside these ranges and needn't reach their ends.
All inputs are finite; a program needn't handle non-finite values.
Results may differ from the reference program's by a relative error of at most 0.0003.
Values sent between devices are 32-bit elements; how exact they have to be, the bound alone decides.
No kernel may reach another device: no remote copies, remote signals or barrier semaphores. Data moves between devices by JAX's collectives and lax.ppermute only.
A program may use at most 128 MiB of HBM per device.

```python
import math
import jax
import jax.numpy as jnp
from jax import lax

NCONF = 65536
TASKS = 128
CAND_DEV = 2048
DIGITS = 10
RADIX = 4
CODES = 1048576
EIG = 8192
CANDS = 32768


def place_ends(result, own_key, smallest, largest):
    longest = result.shape.index(max(result.shape))
    spots = []
    for shift in (0, 1):
        where = [jax.random.randint(jax.random.fold_in(own_key, axis), (), 0, length) for axis, length in enumerate(result.shape)]
        where[longest] = (where[longest] + shift) % result.shape[longest]
        spots.append(tuple(where))
    return result.at[spots[0]].set(smallest).at[spots[1]].set(largest)


def shard_levels(key, dims, shards, least, largest):
    level, own = 1.0, jax.random.fold_in(key, 6)
    for position, parts in shards:
        steps = jnp.exp(jax.random.uniform(jax.random.fold_in(own, position), (parts,), jnp.float32, least / len(shards), largest / len(shards)))
        level = level * jnp.repeat(steps, dims[position] // parts).reshape([-1 if axis == position else 1 for axis in range(len(dims))])
    return level


def gaussian(key, dims, scale, limit, cuts=(), held_as=jnp.bfloat16):
    values = jax.random.normal(key, dims, jnp.float32) * scale
    if len(cuts) > 0:
        values = shard_levels(key, dims, cuts, -0.22, 0.18) * values
    return jnp.clip(values, min=-limit, max=limit).astype(held_as)


def setup_inputs(seed: int = 0) -> dict:
    splits = jax.random.split(jax.random.key(seed), 11)
    basis = gaussian(splits[0], (NCONF, EIG), NCONF ** -0.5, 0.0234375, ((0, 16), (1, 16)), jnp.float32)
    conf_values = jnp.clip(jnp.exp(math.log(8.0) - 2.7725887 * jax.random.uniform(splits[1], (EIG,), jnp.float32) ** shard_levels(splits[1], (EIG,), ((0, 16),), -0.2, 0.2)), 0.5, 8.0)
    task_basis = gaussian(splits[2], (TASKS, TASKS), TASKS ** -0.5, 0.5, (), jnp.float32)
    task_values = jnp.clip(jnp.exp(jax.random.uniform(splits[3], (TASKS,), jnp.float32, math.log(0.5), math.log(4.0))), 0.5, 4.0)
    noise = jnp.clip(jnp.exp(jax.random.uniform(splits[4], (1,), jnp.float32, math.log(0.2), math.log(1.0))), 0.2, 1.0)
    observations = gaussian(splits[5], (NCONF, TASKS), 1.0, 6.0, ((0, 256),), jnp.float32)
    train_codes = place_ends(jax.random.randint(splits[6], (NCONF,), 0, CODES), jax.random.fold_in(splits[6], 1), 0, CODES - 1).astype(jnp.int32)
    length_scales = jnp.clip(jnp.exp(jax.random.uniform(splits[7], (DIGITS,), jnp.float32, math.log(0.03), math.log(0.3))), 0.03, 0.3)
    signal = jnp.clip(jnp.exp(jax.random.uniform(splits[8], (1,), jnp.float32, math.log(0.03), math.log(0.1))), 0.03, 0.1)
    cand_codes = place_ends(jax.random.randint(splits[9], (CANDS,), 0, CODES), jax.random.fold_in(splits[9], 1), 0, CODES - 1).astype(jnp.int32)
    return {"basis": basis, "conf_values": conf_values, "task_basis": task_basis, "task_values": task_values, "noise": noise, "observations": observations, "train_codes": train_codes, "length_scales": length_scales, "signal": signal, "cand_codes": cand_codes}


def decode(codes):
    columns = []
    for place in range(DIGITS):
        columns.append(((codes // (RADIX ** place)) % RADIX).astype(jnp.float32))
    return jnp.stack(columns, axis=1)


def kernel_block(left_digits, right_digits, length_scales, signal):
    total = jnp.zeros((left_digits.shape[0], right_digits.shape[0]), jnp.float32)
    for place in range(DIGITS):
        differ = left_digits[:, place][:, None] - right_digits[:, place][None, :]
        total = total + length_scales[place] * differ * differ
    return signal[0] * jnp.exp(-total)


def reference(basis, conf_values, task_basis, task_values, noise, observations, train_codes, length_scales, signal, cand_codes):
    high = lax.Precision.HIGHEST
    projected = jnp.dot(basis.T, observations, precision=high, preferred_element_type=jnp.float32)
    rotated = jnp.dot(projected, task_basis, precision=high, preferred_element_type=jnp.float32)
    scaled = rotated / (conf_values[:, None] * task_values[None, :] + noise[0])
    back = jnp.dot(scaled, task_basis.T, precision=high, preferred_element_type=jnp.float32)
    coefficients = jnp.dot(basis, back, precision=high, preferred_element_type=jnp.float32)
    task_kernel = jnp.dot(task_basis * task_values[None, :], task_basis.T, precision=high, preferred_element_type=jnp.float32)
    weighted = jnp.dot(coefficients, task_kernel, precision=high, preferred_element_type=jnp.float32)
    train_digits = decode(train_codes)
    blocks = cand_codes.reshape(CANDS // CAND_DEV, CAND_DEV)

    def predict(block_codes):
        cross = kernel_block(decode(block_codes), train_digits, length_scales, signal)
        return jnp.dot(cross, weighted, precision=high, preferred_element_type=jnp.float32)

    means = lax.map(predict, blocks).reshape(CANDS, TASKS)
    return coefficients, means
```

```python
import functools
import math

import jax
import jax.numpy as jnp
from jax import lax
from jax.experimental import pallas as pl
from jax.experimental.pallas import tpu as pltpu
from jax.sharding import PartitionSpec as P

F32 = jnp.float32
BF16 = jnp.bfloat16
VM = pltpu.VMEM
MIB = 1 << 20


def split(x):
    high = x.astype(BF16)
    return high, (x - high.astype(F32)).astype(BF16)


def mul(a, b, dims=(((1,), (0,)), ((), ()))):
    return lax.dot_general(a, b, dims, preferred_element_type=F32)


def mul3(a, b, dims=(((1,), (0,)), ((), ()))):
    ah, al = split(a)
    bh, bl = split(b)
    return mul(ah, bh, dims) + (mul(ah, bl, dims) + mul(al, bh, dims))


NT = (((1,), (1,)), ((), ()))


def swap(value, axis, bits):
    return lax.ppermute(value, axis, [(i, i ^ bits) for i in range(16)])


def full(shape):
    return pl.BlockSpec(shape, lambda *_: (0,) * len(shape))


def params(mib):
    return pltpu.CompilerParams(vmem_limit_bytes=mib * MIB)


def halves_kernel(x, high, low):
    h, l = split(x[...])
    high[...] = h
    low[...] = l


def halves(basis):
    rows, columns = basis.shape
    block = pl.BlockSpec((512, columns), lambda i: (i, 0))
    return pl.pallas_call(
        halves_kernel,
        grid=(rows // 512,),
        in_specs=[block],
        out_specs=[block, block],
        out_shape=[jax.ShapeDtypeStruct(basis.shape, BF16)] * 2,
        compiler_params=params(8),
        cost_estimate=pl.CostEstimate(flops=0, bytes_accessed=16 * MIB, transcendentals=0),
        name="basis_halves",
    )(basis)


def project_kernel(where, high, low, task_basis, *refs):
    blocks, out = refs[:8], refs[8]
    me = where[0]
    total = jnp.zeros(out.shape, F32)
    for group in range(8):
        for far in range(2):
            slot = (group % 4) * 2 + group // 4 + far * 8
            rows = pl.ds(pl.multiple_of((me ^ slot) * 256, 256), 256)
            oh, ol = split(blocks[group][far, 0:128, :])
            bh = high[rows, :]
            both = mul(jnp.concatenate([oh, ol], axis=0), bh)
            total = total + both[:128] + (both[128:] + mul(oh, low[rows, :]))
    out[...] = mul3(task_basis[...].T, total)


def project(where, high, low, task_basis, blocks):
    return pl.pallas_call(
        project_kernel,
        in_specs=[pl.BlockSpec(memory_space=pltpu.SMEM)] + [pl.BlockSpec(memory_space=VM)] * 11,
        out_specs=pl.BlockSpec(memory_space=VM),
        out_shape=jax.ShapeDtypeStruct((128, high.shape[1]), F32),
        compiler_params=params(24),
        cost_estimate=pl.CostEstimate(flops=6 * 4096 * 512 * 128, bytes_accessed=10 * MIB, transcendentals=0),
        name="project",
    )(where, high, low, task_basis, *blocks)


def scale_kernel(where, noise, pieces, conf_values, task_values, out):
    rows = pl.ds(pl.multiple_of(where[1] * 8, 8), 8)
    total = jnp.sum(pieces[...], axis=0)
    scaled = total / (conf_values[...] * task_values[rows, :] + noise[0])
    out[...] = jnp.broadcast_to(scaled[None], out.shape)


def scale(where, noise, pieces, conf_values, task_values):
    smem = pl.BlockSpec(memory_space=pltpu.SMEM)
    return pl.pallas_call(
        scale_kernel,
        in_specs=[smem, smem] + [pl.BlockSpec(memory_space=VM)] * 3,
        out_specs=pl.BlockSpec(memory_space=VM),
        out_shape=jax.ShapeDtypeStruct(pieces.shape, F32),
        compiler_params=params(4),
        name="scale",
    )(where, noise, pieces, conf_values, task_values)


def expand_kernel(where, high, low, task_basis, scaled, *outs):
    me = where[0]
    back = mul3(scaled[...].T, task_basis[...], NT)
    kh, kl = split(back)
    wide = jnp.concatenate([kh, kl], axis=1)
    for group in (5, 6, 7, 4, 1, 2, 3, 0):
        for far in range(2):
            slot = (group % 4) * 2 + group // 4 + far * 8
            rows = pl.ds(pl.multiple_of((me ^ slot) * 256, 256), 256)
            both = mul(high[rows, :], wide)
            outs[group][far] = both[:, :128] + (both[:, 128:] + mul(low[rows, :], kh))


def expand(where, high, low, task_basis, scaled):
    return pl.pallas_call(
        expand_kernel,
        in_specs=[pl.BlockSpec(memory_space=pltpu.SMEM)] + [pl.BlockSpec(memory_space=VM)] * 4,
        out_specs=[pl.BlockSpec(memory_space=VM)] * 8,
        out_shape=[jax.ShapeDtypeStruct((2, 256, 128), F32)] * 8,
        compiler_params=params(24),
        cost_estimate=pl.CostEstimate(flops=6 * 4096 * 512 * 128, bytes_accessed=10 * MIB, transcendentals=0),
        name="expand",
    )(where, high, low, task_basis, scaled)


def row_digit(codes, k):
    part = (k >= 40).astype(jnp.int32) + (k >= 80).astype(jnp.int32) + (k >= 120).astype(jnp.int32)
    rest = k - 40 * part
    return part, rest & 3, lax.shift_right_logical(codes, 2 * lax.shift_right_logical(rest, 2)) & 3


def onehot_kernel(where, codes, out):
    k = lax.broadcasted_iota(jnp.int32, (128, 128), 0)
    for slot in range(16):
        row = codes[where[1] ^ slot, pl.ds(0, 1), :].astype(jnp.int32)
        _, level, digit = row_digit(jnp.broadcast_to(row, (128, 128)), k)
        hot = jnp.where(digit == level, 1.0, 0.0).astype(F32)
        out[slot * 128 : slot * 128 + 128, :] = hot.T.astype(BF16)


def onehot(where, codes):
    return pl.pallas_call(
        onehot_kernel,
        in_specs=[pl.BlockSpec(memory_space=pltpu.SMEM), pl.BlockSpec(memory_space=VM)],
        out_specs=pl.BlockSpec(memory_space=VM),
        out_shape=jax.ShapeDtypeStruct((2048, 128), BF16),
        compiler_params=params(4),
        name="candidate_levels",
    )(where, codes)


def cross_kernel(hot, codes, lengths, high, low, table):
    @pl.when(pl.program_id(0) == 0)
    def _():
        k = lax.broadcasted_iota(jnp.int32, (128, 256), 0)
        length = jnp.concatenate([lengths[...], lengths[...]], axis=1)
        for far in range(2):
            row = codes[far, 0:1, :].astype(jnp.int32)
            part, level, digit = row_digit(jnp.broadcast_to(row, (128, 256)), k)
            differ = (level - digit).astype(F32)
            value = length * differ * differ
            first = value.astype(BF16).astype(F32)
            second = (value - first).astype(BF16).astype(F32)
            third = value - first - second
            piece = jnp.where(part == 0, first, jnp.where(part == 1, second, jnp.where(part == 2, third, 0.0)))
            table[:, far * 256 : far * 256 + 256] = piece.astype(BF16)

    cross = jnp.exp2(mul(hot[...], table[...]))
    h, l = split(cross)
    high[...] = h
    low[...] = l


def cross_halves(hot, block, lengths):
    rows = hot.shape[0]
    step = 256
    out = pl.BlockSpec((step, 512), lambda i: (i, 0))
    return pl.pallas_call(
        cross_kernel,
        grid=(rows // step,),
        in_specs=[
            pl.BlockSpec((step, 128), lambda i: (i, 0)),
            pl.BlockSpec((2, 8, 256), lambda i: (0, 16, 0)),
            full((128, 128)),
        ],
        out_specs=[out, out],
        out_shape=[jax.ShapeDtypeStruct((rows, 512), BF16)] * 2,
        scratch_shapes=[pltpu.VMEM((128, 512), BF16)],
        compiler_params=params(8),
        cost_estimate=pl.CostEstimate(flops=2 * 2048 * 512 * 128, bytes_accessed=5 * MIB, transcendentals=2048 * 512),
        name="cross",
    )(hot, block, lengths)


def predict_kernel(near, other, h0, l0, h1, l1, *refs):
    total, out, wide = (refs[0] if len(refs) == 3 else None), refs[-2], refs[-1]

    @pl.when(pl.program_id(0) == 0)
    def _():
        for place, ref in enumerate((near, other)):
            for far in range(2):
                rows = pl.ds(place * 512 + far * 256, 256)
                wh, wl = split(ref[far])
                wide[rows, 0:128] = wh
                wide[rows, 128:256] = wl

    both = mul(h0[...], wide[0:512, :]) + mul(h1[...], wide[512:1024, :])
    rest = mul(l0[...], wide[0:512, 0:128]) + mul(l1[...], wide[512:1024, 0:128])
    value = both[:, :128] + (both[:, 128:] + rest)
    out[...] = value if total is None else total[...] + value


def predict(near, other, cross0, cross1, total, first, count):
    step = 256
    base = first // step
    block = pl.BlockSpec((step, 512), lambda i: (base + i, 0))
    out = pl.BlockSpec((step, 128), lambda i: (i, 0))
    extra, extra_specs = ([], []) if total is None else ([total], [pl.BlockSpec((step, 128), lambda i: (base + i, 0))])
    return pl.pallas_call(
        predict_kernel,
        grid=(count // step,),
        in_specs=[full((2, 256, 128))] * 2 + [block] * 4 + extra_specs,
        out_specs=out,
        out_shape=jax.ShapeDtypeStruct((count, 128), F32),
        scratch_shapes=[pltpu.VMEM((1024, 256), BF16)],
        compiler_params=params(10),
        cost_estimate=pl.CostEstimate(flops=6 * count * 1024 * 128, bytes_accessed=count * 4096 + count * 1024, transcendentals=0),
        name="predict",
    )(near, other, *cross0, *cross1, *extra)


def finish_kernel(signal, a, b, c, d, task_basis, task_values, out):
    kernel = mul3(task_basis[...] * task_values[...], task_basis[...], NT)
    out[...] = signal[0] * mul3(a[...] + b[...] + c[...] + d[...], kernel)


def finish(signal, parts, task_basis, task_values):
    return pl.pallas_call(
        finish_kernel,
        in_specs=[pl.BlockSpec(memory_space=pltpu.SMEM)] + [pl.BlockSpec(memory_space=VM)] * 6,
        out_specs=pl.BlockSpec(memory_space=VM),
        out_shape=jax.ShapeDtypeStruct((128, 128), F32),
        compiler_params=params(4),
        name="finish",
    )(signal, *parts, task_basis, task_values)


def local(
    basis,
    conf_values,
    task_basis,
    task_values,
    noise,
    observations,
    train_codes,
    length_scales,
    signal,
    cand_codes,
):
    n = lax.axis_index("narrow").astype(jnp.int32)
    w = lax.axis_index("wide").astype(jnp.int32)
    where = jnp.stack([n, w])
    high, low = halves(basis)

    own = jnp.concatenate(
        [observations.T, jnp.broadcast_to(train_codes.astype(F32)[None], (8, 256))], axis=0
    )
    pair = jnp.stack([own, swap(own, "narrow", 8)])
    near = [pair] + [swap(pair, "narrow", 2 * d) for d in (1, 2, 3)]
    other = [swap(block, "narrow", 1) for block in near]
    blocks = near + other

    own_codes = lax.dynamic_slice(cand_codes, (n * 128,), (128,)).astype(F32)
    codes = lax.all_to_all(jnp.broadcast_to(own_codes, (16, 8, 128)), "wide", 0, 0)
    hot = onehot(where, codes)
    exponents = jnp.repeat(length_scales * (-1.0 / math.log(2.0)), 4)
    exponents = jnp.concatenate([exponents, exponents, exponents, jnp.zeros((8,), F32)])
    lengths = jnp.broadcast_to(exponents[:, None], (128, 128))
    crosses = [cross_halves(hot, block, lengths) for block in blocks]

    rotated = project(where, high, low, task_basis, blocks)
    pieces = lax.all_to_all(rotated.reshape(16, 8, -1), "wide", 0, 0)
    scaled = scale(where, noise, pieces, conf_values[None], task_values[:, None])
    scaled = lax.all_to_all(scaled, "wide", 0, 0).reshape(128, -1)

    parts = expand(where, high, low, task_basis, scaled)
    sums = {}
    for d in (1, 2, 3, 0):
        sums[d] = parts[d] + swap(parts[4 + d], "narrow", 1)
    total = sums[0]
    for d in (1, 2, 3):
        total = total + swap(sums[d], "narrow", 2 * d)
    mirror = swap(total, "narrow", 8)
    total = total + mirror[::-1]
    coefficients = total[0]

    weights = [total] + [swap(total, "narrow", 2 * d) for d in (1, 2, 3)]
    others = [swap(block, "narrow", 1) for block in weights]
    means = None
    for d in (0, 1, 2):
        means = predict(weights[d], others[d], crosses[d], crosses[4 + d], means, 0, 2048)
    last = {}
    for g in (1, 2, 3, 0):
        last[g] = predict(weights[3], others[3], crosses[3], crosses[7], means, g * 512, 512)
    block = last[0]
    for g in (1, 2, 3):
        block = block + swap(last[g], "wide", 4 * g)
    quarters = block.reshape(4, 128, 128)
    ends = [quarters[0]] + [swap(quarters[g], "wide", g) for g in (1, 2, 3)]
    return coefficients, finish(signal, ends, task_basis, task_values[None])


def solution(mesh):
    return jax.shard_map(
        local,
        mesh=mesh,
        in_specs=(
            P("wide", "narrow"),
            P("narrow"),
            P(),
            P(),
            P(),
            P(("wide", "narrow"), None),
            P(("wide", "narrow")),
            P(),
            P(),
            P("wide"),
        ),
        out_specs=(P(("wide", "narrow"), None), P(("wide", "narrow"), None)),
        check_vma=False,
    )
```

```python
import functools
import math

import jax
import jax.numpy as jnp
from jax import lax
from jax.experimental import pallas as pl
from jax.experimental.pallas import tpu as pltpu
from jax.sharding import PartitionSpec as P

F32 = jnp.float32
BF16 = jnp.bfloat16
VM = pltpu.VMEM
MIB = 1 << 20


def far_memory(value):
    return pltpu.with_memory_space_constraint(value, pltpu.HBM)


def split(x):
    high = x.astype(BF16)
    return high, (x - high.astype(F32)).astype(BF16)


def mul(a, b, dims=(((1,), (0,)), ((), ()))):
    return lax.dot_general(a, b, dims, preferred_element_type=F32)


def mul3(a, b, dims=(((1,), (0,)), ((), ()))):
    ah, al = split(a)
    bh, bl = split(b)
    return mul(ah, bh, dims) + (mul(ah, bl, dims) + mul(al, bh, dims))


NT = (((1,), (1,)), ((), ()))


def swap(value, axis, bits):
    return lax.ppermute(value, axis, [(i, i ^ bits) for i in range(16)])


def full(shape):
    return pl.BlockSpec(shape, lambda *_: (0,) * len(shape))


def params(mib):
    return pltpu.CompilerParams(vmem_limit_bytes=mib * MIB)


def here(count):
    return [pl.BlockSpec(memory_space=VM)] * count


def scalars(count):
    return [pl.BlockSpec(memory_space=pltpu.SMEM)] * count


def anywhere(count):
    return [pl.BlockSpec(memory_space=pl.ANY)] * count


def struct(shape, dtype=F32):
    return jax.ShapeDtypeStruct(shape, dtype)


def cost(flops=0, moved=0, transcendentals=0):
    return pl.CostEstimate(flops=flops, bytes_accessed=moved, transcendentals=transcendentals)


def halves_kernel(basis, high, low, held, arrived):
    def fetch(step):
        rows = pl.ds(step * 512, 512)
        return pltpu.make_async_copy(basis.at[rows, :], held.at[step % 2], arrived.at[step % 2])

    fetch(0).start()
    for step in range(8):
        if step < 7:
            fetch(step + 1).start()
        fetch(step).wait()
        h, l = split(held[step % 2])
        high[step * 512 : step * 512 + 512, :] = h
        low[step * 512 : step * 512 + 512, :] = l


def halves(basis):
    return pl.pallas_call(
        halves_kernel,
        in_specs=anywhere(1),
        out_specs=here(2),
        out_shape=[struct((4096, 512), BF16)] * 2,
        scratch_shapes=[pltpu.VMEM((2, 512, 512), F32), pltpu.SemaphoreType.DMA((2,))],
        compiler_params=params(12),
        cost_estimate=cost(0, 16 * MIB),
        name="basis_halves",
    )(far_memory(basis))


def gate_kernel(value, *refs):
    refs[-1][...] = value[...]


def gate(value, after):
    return pl.pallas_call(
        gate_kernel,
        in_specs=here(1) + anywhere(len(after)),
        out_specs=here(1)[0],
        out_shape=struct(value.shape),
        compiler_params=params(2),
        name="gate",
    )(value, *after)


def own_kernel(where, observations, codes, out):
    out[0:128, :] = observations[...].T
    out[128:136, :] = jnp.broadcast_to(codes[...].astype(F32), (8, 256))


def own_block(where, observations, codes):
    return pl.pallas_call(
        own_kernel,
        grid=(1,),
        in_specs=scalars(1) + [full((256, 128)), full((1, 256))],
        out_specs=full((136, 256)),
        out_shape=struct((136, 256)),
        compiler_params=params(2),
        name="own_observations",
    )(where, far_memory(observations), far_memory(codes[None]))


def project_part(me, high, low, blocks, far):
    total = jnp.zeros((128, 512), F32)
    for group in range(8):
        slot = (group % 4) * 2 + group // 4 + far * 8
        rows = pl.ds(pl.multiple_of((me ^ slot) * 256, 256), 256)
        oh, ol = split(blocks[group][0:128, :])
        both = mul(jnp.concatenate([oh, ol], axis=0), high[rows, :])
        total = total + both[:128] + (both[128:] + mul(oh, low[rows, :]))
    return total


def near_kernel(where, high, low, *refs):
    refs[8][...] = project_part(where[0], high, low, refs[:8], 0)


def project_near(where, high, low, blocks):
    return pl.pallas_call(
        near_kernel,
        in_specs=scalars(1) + here(10),
        out_specs=here(1)[0],
        out_shape=struct((128, 512)),
        compiler_params=params(16),
        cost_estimate=cost(3 * 4096 * 512 * 128, 5 * MIB),
        name="project_near",
    )(where, high, low, *blocks)


def project_kernel(where, high, low, task_basis, cand, before, *refs):
    blocks, outs, rotated = refs[:8], refs[8:12], refs[12]
    me, x = where[0], where[1] // 4
    total = before[...] + project_part(me, high, low, blocks, 1)
    rotated[...] = mul3(task_basis[...].T, total)
    columns = pl.ds(pl.multiple_of(me * 128, 128), 128)
    codes = jnp.broadcast_to(cand[:, columns].astype(F32), (8, 128))
    for d in range(4):
        outs[d][0:32, :] = rotated[pl.ds(pl.multiple_of((x ^ d) * 32, 32), 32), :]
        outs[d][32:40, :] = jnp.concatenate([codes] * 4, axis=1)


def project(where, high, low, task_basis, cand, before, blocks):
    return pl.pallas_call(
        project_kernel,
        in_specs=scalars(1) + here(13),
        out_specs=here(4),
        out_shape=[struct((40, 512))] * 4,
        scratch_shapes=[pltpu.VMEM((128, 512), F32)],
        compiler_params=params(16),
        cost_estimate=cost(3 * 4096 * 512 * 128, 5 * MIB),
        name="project",
    )(where, high, low, task_basis, cand, before, *blocks)


def collect_kernel(own, a, b, c, out):
    out[0:32, :] = (own[0:32, :] + a[0:32, :]) + (b[0:32, :] + c[0:32, :])
    rows = [ref[32:33, :] for ref in (own, a, b, c)]
    out[32:40, :] = jnp.concatenate(rows + rows, axis=0)


def collect(pieces):
    return pl.pallas_call(
        collect_kernel,
        in_specs=here(4),
        out_specs=here(1)[0],
        out_shape=struct((40, 512)),
        compiler_params=params(2),
        name="sum_over_x",
    )(*pieces)


def scale_kernel(where, noise, conf_values, task_values, own, a, b, c, out, codes, column):
    column[...] = jnp.broadcast_to(task_values[...], (128, 128)).T
    rows = pl.ds(pl.multiple_of(where[1] // 4 * 32, 32), 32)
    total = (own[0:32, :] + a[0:32, :]) + (b[0:32, :] + c[0:32, :])
    out[...] = total / (conf_values[...] * column[rows, 0:1] + noise[0])
    for far in range(4):
        for near, ref in enumerate((own, a, b, c)):
            slot = far * 4 + near
            codes[slot : slot + 1, :] = ref[32 + far : 33 + far, 0:128]


def scale(where, noise, conf_values, task_values, pieces):
    return pl.pallas_call(
        scale_kernel,
        in_specs=scalars(2) + here(6),
        out_specs=here(2),
        out_shape=[struct((32, 512)), struct((16, 128))],
        scratch_shapes=[pltpu.VMEM((128, 128), F32)],
        compiler_params=params(2),
        name="scale",
    )(where, noise, conf_values, task_values, *pieces)


def back_kernel(where, task_basis, a, b, c, d, *refs):
    out, scaled = refs[-2:]
    x = where[1] // 4
    for far, ref in enumerate((a, b, c, d)):
        scaled[pl.ds(pl.multiple_of((x ^ far) * 32, 32), 32), :] = ref[...]
    kh, kl = split(mul3(scaled[...].T, task_basis[...], NT))
    out[:, 0:128] = kh
    out[:, 128:256] = kl


def rotate_back(where, task_basis, pieces, after):
    return pl.pallas_call(
        back_kernel,
        in_specs=scalars(1) + here(5) + anywhere(len(after)),
        out_specs=here(1)[0],
        out_shape=struct((512, 256), BF16),
        scratch_shapes=[pltpu.VMEM((128, 512), F32)],
        compiler_params=params(4),
        name="rotate_back",
    )(where, task_basis, *pieces, *after)


def expand_kernel(d, where, high, low, wide, odd, even):
    me = where[0]
    for core, out in ((1, odd), (0, even)):
        for far in range(2):
            slot = d * 2 + core + far * 8
            rows = pl.ds(pl.multiple_of((me ^ slot) * 256, 256), 256)
            both = mul(high[rows, :], wide[...])
            out[far] = both[:, :128] + (both[:, 128:] + mul(low[rows, :], wide[:, 0:128]))


def expand(d, where, high, low, wide):
    return pl.pallas_call(
        functools.partial(expand_kernel, d),
        in_specs=scalars(1) + here(3),
        out_specs=here(2),
        out_shape=[struct((2, 256, 128))] * 2,
        compiler_params=params(12),
        cost_estimate=cost(6 * 1024 * 512 * 128, 3 * MIB),
        name="expand",
    )(where, high, low, wide)


def sum_kernel(a, b, c, d, *refs):
    refs[-1][...] = (a[...] + b[...]) + (c[...] + d[...])


def sum_blocks(blocks, after):
    return pl.pallas_call(
        sum_kernel,
        in_specs=here(4) + anywhere(len(after)),
        out_specs=here(1)[0],
        out_shape=struct((2, 256, 128)),
        compiler_params=params(2),
        name="sum_over_y",
    )(*blocks, *after)


def mirror_kernel(a, b, *refs):
    refs[-1][0] = a[0] + b[1]
    refs[-1][1] = a[1] + b[0]


def sum_mirror(mine, theirs, after):
    return pl.pallas_call(
        mirror_kernel,
        in_specs=here(2) + anywhere(len(after)),
        out_specs=here(1)[0],
        out_shape=struct((2, 256, 128)),
        compiler_params=params(2),
        name="sum_over_far",
    )(mine, theirs, *after)


def row_digit(codes, k):
    part = (k >= 40).astype(jnp.int32) + (k >= 80).astype(jnp.int32) + (k >= 120).astype(jnp.int32)
    rest = k - 40 * part
    return part, rest & 3, lax.shift_right_logical(codes, 2 * lax.shift_right_logical(rest, 2)) & 3


def onehot_kernel(length_scales, codes, out, lengths):
    k = lax.broadcasted_iota(jnp.int32, (128, 128), 0)
    part, _, _ = row_digit(k, k)
    feature = lax.shift_right_logical(k - 40 * part, 2)
    value = jnp.zeros((128, 128), F32)
    for place in range(10):
        value = jnp.where(feature == place, length_scales[place] * (-1.0 / math.log(2.0)), value)
    lengths[...] = value
    for slot in range(16):
        row = codes[slot : slot + 1, :].astype(jnp.int32)
        _, level, digit = row_digit(jnp.broadcast_to(row, (128, 128)), k)
        hot = jnp.where(digit == level, 1.0, 0.0).astype(F32)
        out[slot * 128 : slot * 128 + 128, :] = hot.T.astype(BF16)


def onehot(length_scales, codes):
    return pl.pallas_call(
        onehot_kernel,
        in_specs=scalars(1) + here(1),
        out_specs=here(2),
        out_shape=[struct((2048, 128), BF16), struct((128, 128))],
        compiler_params=params(2),
        name="candidate_levels",
    )(length_scales, codes)


def cross_kernel(hot, codes0, codes1, lengths, high, low):
    k = lax.broadcasted_iota(jnp.int32, (128, 256), 0)
    length = jnp.concatenate([lengths[...], lengths[...]], axis=1)
    tables = []
    for codes in (codes0, codes1):
        row = codes[128:129, :].astype(jnp.int32)
        part, level, digit = row_digit(jnp.broadcast_to(row, (128, 256)), k)
        differ = (level - digit).astype(F32)
        value = length * differ * differ
        first = value.astype(BF16).astype(F32)
        second = (value - first).astype(BF16).astype(F32)
        third = value - first - second
        piece = jnp.where(part == 0, first, jnp.where(part == 1, second, jnp.where(part == 2, third, 0.0)))
        tables.append(piece.astype(BF16))
    table = jnp.concatenate(tables, axis=1)
    for step in range(8):
        rows = pl.ds(step * 256, 256)
        h, l = split(jnp.exp2(mul(hot[rows, :], table)))
        high[rows, :] = h
        low[rows, :] = l


def cross_halves(hot, block0, block1, lengths):
    return pl.pallas_call(
        cross_kernel,
        in_specs=here(4),
        out_specs=here(2),
        out_shape=[struct((2048, 512), BF16)] * 2,
        compiler_params=params(8),
        cost_estimate=cost(2 * 2048 * 512 * 128, 5 * MIB, 2048 * 512),
        name="cross",
    )(hot, block0, block1, lengths)


def predict_kernel(first, near, other, h0, l0, h1, l1, *refs):
    total, out, wide = (refs[0] if len(refs) == 3 else None), refs[-2], refs[-1]
    for place, ref in enumerate((near, other)):
        for far in range(2):
            rows = pl.ds(place * 512 + far * 256, 256)
            wh, wl = split(ref[far])
            wide[rows, 0:128] = wh
            wide[rows, 128:256] = wl
    for step in range(out.shape[0] // 256):
        rows, to = pl.ds(first + step * 256, 256), pl.ds(step * 256, 256)
        both = mul(h0[rows, :], wide[0:512, :]) + mul(h1[rows, :], wide[512:1024, :])
        rest = mul(l0[rows, :], wide[0:512, 0:128]) + mul(l1[rows, :], wide[512:1024, 0:128])
        value = both[:, :128] + (both[:, 128:] + rest)
        out[to, :] = value if total is None else total[rows, :] + value


def predict(near, other, cross0, cross1, total, first, count):
    extra = [] if total is None else [total]
    return pl.pallas_call(
        functools.partial(predict_kernel, first),
        in_specs=here(6 + len(extra)),
        out_specs=here(1)[0],
        out_shape=struct((count, 128)),
        scratch_shapes=[pltpu.VMEM((1024, 256), BF16)],
        compiler_params=params(14),
        cost_estimate=cost(48 * count * 1024 * 128, count * 5120),
        name="predict",
    )(near, other, *cross0, *cross1, *extra)


def quarter_kernel(a, b, c, d, *outs):
    for g in range(4):
        rows = pl.ds(g * 128, 128)
        outs[g][...] = (a[rows, :] + b[rows, :]) + (c[rows, :] + d[rows, :])


def sum_quarters(blocks):
    return pl.pallas_call(
        quarter_kernel,
        in_specs=here(4),
        out_specs=here(4),
        out_shape=[struct((128, 128))] * 4,
        compiler_params=params(3),
        name="means_over_x",
    )(*blocks)


def finish_kernel(signal, a, b, c, d, task_basis, task_values, out):
    kernel = mul3(task_basis[...] * task_values[...], task_basis[...], NT)
    out[...] = signal[0] * mul3((a[...] + b[...]) + (c[...] + d[...]), kernel)


def finish(signal, parts, task_basis, task_values):
    return pl.pallas_call(
        finish_kernel,
        in_specs=scalars(1) + here(6),
        out_specs=here(1)[0],
        out_shape=struct((128, 128)),
        compiler_params=params(2),
        name="finish",
    )(signal, *parts, task_basis, task_values)


def local(
    basis,
    conf_values,
    task_basis,
    task_values,
    noise,
    observations,
    train_codes,
    length_scales,
    signal,
    cand_codes,
):
    n = lax.axis_index("narrow").astype(jnp.int32)
    w = lax.axis_index("wide").astype(jnp.int32)
    where = jnp.stack([n, w])

    own = own_block(where, observations, train_codes)
    high, low = halves(basis)
    mirror = gate(swap(own, "narrow", 8), [high])
    blocks = []
    for first in (own, mirror):
        near = [first] + [swap(first, "narrow", 2 * d) for d in (1, 2, 3)]
        blocks += near + [swap(block, "narrow", 1) for block in near]

    before = project_near(where, high, low, blocks[:8])
    pieces = project(where, high, low, task_basis, cand_codes[None], before, blocks[8:])
    mine = collect([pieces[0]] + [swap(pieces[d], "wide", 4 * d) for d in (1, 2, 3)])
    arrived = [mine] + [swap(mine, "wide", d) for d in (1, 2, 3)]
    scaled, codes = scale(where, noise, conf_values[None], task_values[None], arrived)
    quarters = [scaled] + [swap(scaled, "wide", 4 * d) for d in (1, 2, 3)]

    hot, lengths = onehot(length_scales, codes)
    crosses = [cross_halves(hot, blocks[g], blocks[8 + g], lengths) for g in range(8)]

    wide = rotate_back(where, task_basis, quarters, [crosses[g][0] for g in (0, 4, 1)])
    sums = {}
    for d in (1, 2, 3, 0):
        odd, even = expand(d, where, high, low, wide)
        sums[d] = even + swap(odd, "narrow", 1)
    total = [sums[0]] + [swap(sums[d], "narrow", 2 * d) for d in (1, 2, 3)]
    total = sum_blocks(total, [crosses[g][0] for g in (5, 2, 6)])
    total = sum_mirror(total, swap(total, "narrow", 8), [crosses[g][0] for g in (3, 7)])
    coefficients = total[0]

    weights = [total] + [swap(total, "narrow", 2 * d) for d in (1, 2, 3)]
    means, done = None, []
    for d in range(4):
        near = gate(weights[d], done[d - 2 : d - 1]) if d >= 2 else weights[d]
        other = swap(near, "narrow", 1)
        if d < 3:
            means = predict(near, other, crosses[d], crosses[4 + d], means, 0, 2048)
            done.append(means)
    last = {}
    for g in (1, 2, 3, 0):
        last[g] = predict(near, other, crosses[3], crosses[7], means, g * 512, 512)
    quarters = sum_quarters([last[0]] + [swap(last[g], "wide", 4 * g) for g in (1, 2, 3)])
    ends = [quarters[0]] + [swap(quarters[g], "wide", g) for g in (1, 2, 3)]
    return coefficients, finish(signal, ends, task_basis, task_values[None])


def solution(mesh):
    return jax.shard_map(
        local,
        mesh=mesh,
        in_specs=(
            P("wide", "narrow"),
            P("narrow"),
            P(),
            P(),
            P(),
            P(("wide", "narrow"), None),
            P(("wide", "narrow")),
            P(),
            P(),
            P("wide"),
        ),
        out_specs=(P(("wide", "narrow"), None), P(("wide", "narrow"), None)),
        check_vma=False,
    )
```

```python
import functools
import math

import jax
import jax.numpy as jnp
from jax import lax
from jax.experimental import pallas as pl
from jax.experimental.pallas import tpu as pltpu
from jax.sharding import PartitionSpec as P

F32 = jnp.float32
BF16 = jnp.bfloat16
VM = pltpu.VMEM
MIB = 1 << 20


def far_memory(value):
    return pltpu.with_memory_space_constraint(value, pltpu.HBM)


def split(x):
    high = x.astype(BF16)
    return high, (x - high.astype(F32)).astype(BF16)


def mul(a, b, dims=(((1,), (0,)), ((), ()))):
    return lax.dot_general(a, b, dims, preferred_element_type=F32)


def mul3(a, b, dims=(((1,), (0,)), ((), ()))):
    ah, al = split(a)
    bh, bl = split(b)
    return mul(ah, bh, dims) + (mul(ah, bl, dims) + mul(al, bh, dims))


NT = (((1,), (1,)), ((), ()))


def swap(value, axis, bits):
    return lax.ppermute(value, axis, [(i, i ^ bits) for i in range(16)])


def full(shape):
    return pl.BlockSpec(shape, lambda *_: (0,) * len(shape))


def params(mib):
    return pltpu.CompilerParams(vmem_limit_bytes=mib * MIB)


def here(count):
    return [pl.BlockSpec(memory_space=VM)] * count


def scalars(count):
    return [pl.BlockSpec(memory_space=pltpu.SMEM)] * count


def anywhere(count):
    return [pl.BlockSpec(memory_space=pl.ANY)] * count


def struct(shape, dtype=F32):
    return jax.ShapeDtypeStruct(shape, dtype)


def cost(flops=0, moved=0, transcendentals=0):
    return pl.CostEstimate(flops=flops, bytes_accessed=moved, transcendentals=transcendentals)


def halves_kernel(basis, high, low, held, arrived):
    def fetch(step):
        rows = pl.ds(pl.multiple_of(step * 512, 512), 512)
        return pltpu.make_async_copy(basis.at[rows, :], held.at[rows, :], arrived.at[step])

    for step in range(8):
        fetch(step).start()

    def part(step, carry):
        fetch(step).wait()
        rows = pl.ds(pl.multiple_of(step * 512, 512), 512)
        h, l = split(held[rows, :])
        high[rows, :] = h
        low[rows, :] = l
        return carry

    lax.fori_loop(0, 8, part, 0)


def halves(basis):
    return pl.pallas_call(
        halves_kernel,
        in_specs=anywhere(1),
        out_specs=here(2),
        out_shape=[struct((4096, 512), BF16)] * 2,
        scratch_shapes=[pltpu.VMEM((4096, 512), F32), pltpu.SemaphoreType.DMA((8,))],
        compiler_params=params(20),
        cost_estimate=cost(1, 1),
        name="basis_halves",
    )(far_memory(basis))


def gate_kernel(value, *refs):
    refs[-1][...] = value[...]


def gate(value, after):
    return pl.pallas_call(
        gate_kernel,
        in_specs=here(1) + anywhere(len(after)),
        out_specs=here(1)[0],
        out_shape=struct(value.shape),
        compiler_params=params(2),
        name="gate",
    )(value, *after)


def own_kernel(where, observations, codes, out):
    out[0:128, :] = observations[...].T
    out[128:136, :] = jnp.broadcast_to(codes[...].astype(F32), (8, 256))


def own_block(where, observations, codes):
    return pl.pallas_call(
        own_kernel,
        grid=(1,),
        in_specs=scalars(1) + [full((256, 128)), full((1, 256))],
        out_specs=full((136, 256)),
        out_shape=struct((136, 256)),
        compiler_params=params(2),
        name="own_observations",
    )(where, far_memory(observations), far_memory(codes[None]))


def project_part(me, high, low, blocks, far):
    total = jnp.zeros((128, 512), F32)
    for group in range(8):
        slot = (group % 4) * 2 + group // 4 + far * 8
        rows = pl.ds(pl.multiple_of((me ^ slot) * 256, 256), 256)
        oh, ol = split(blocks[group][0:128, :])
        both = mul(jnp.concatenate([oh, ol], axis=0), high[rows, :])
        total = total + both[:128] + (both[128:] + mul(oh, low[rows, :]))
    return total


def near_kernel(where, high, low, *refs):
    refs[8][...] = project_part(where[0], high, low, refs[:8], 0)


def project_near(where, high, low, blocks):
    return pl.pallas_call(
        near_kernel,
        in_specs=scalars(1) + here(10),
        out_specs=here(1)[0],
        out_shape=struct((128, 512)),
        compiler_params=params(16),
        cost_estimate=cost(1, 1),
        name="project_near",
    )(where, high, low, *blocks)


def project_kernel(where, high, low, task_basis, cand, before, *refs):
    blocks, outs, rotated = refs[:8], refs[8:12], refs[12]
    me, x = where[0], where[1] // 4
    total = before[...] + project_part(me, high, low, blocks, 1)
    rotated[...] = mul3(task_basis[...].T, total)
    columns = pl.ds(pl.multiple_of(me * 128, 128), 128)
    codes = jnp.broadcast_to(cand[:, columns].astype(F32), (8, 128))
    for d in range(4):
        outs[d][0:32, :] = rotated[pl.ds(pl.multiple_of((x ^ d) * 32, 32), 32), :]
        outs[d][32:40, :] = jnp.concatenate([codes] * 4, axis=1)


def project(where, high, low, task_basis, cand, before, blocks):
    return pl.pallas_call(
        project_kernel,
        in_specs=scalars(1) + here(13),
        out_specs=here(4),
        out_shape=[struct((40, 512))] * 4,
        scratch_shapes=[pltpu.VMEM((128, 512), F32)],
        compiler_params=params(16),
        cost_estimate=cost(1, 1),
        name="project",
    )(where, high, low, task_basis, cand, before, *blocks)


def collect_kernel(own, a, b, c, out):
    out[0:32, :] = (own[0:32, :] + a[0:32, :]) + (b[0:32, :] + c[0:32, :])
    rows = [ref[32:33, :] for ref in (own, a, b, c)]
    out[32:40, :] = jnp.concatenate(rows + rows, axis=0)


def collect(pieces):
    return pl.pallas_call(
        collect_kernel,
        in_specs=here(4),
        out_specs=here(1)[0],
        out_shape=struct((40, 512)),
        compiler_params=params(2),
        name="sum_over_x",
    )(*pieces)


def scale_kernel(where, noise, conf_values, task_values, own, a, b, c, out, codes, column):
    column[...] = jnp.broadcast_to(task_values[...], (128, 128)).T
    rows = pl.ds(pl.multiple_of(where[1] // 4 * 32, 32), 32)
    total = (own[0:32, :] + a[0:32, :]) + (b[0:32, :] + c[0:32, :])
    out[...] = total / (conf_values[...] * column[rows, 0:1] + noise[0])
    for far in range(4):
        for near, ref in enumerate((own, a, b, c)):
            slot = far * 4 + near
            codes[slot : slot + 1, :] = ref[32 + far : 33 + far, 0:128]


def scale(where, noise, conf_values, task_values, pieces):
    return pl.pallas_call(
        scale_kernel,
        in_specs=scalars(2) + here(6),
        out_specs=here(2),
        out_shape=[struct((32, 512)), struct((16, 128))],
        scratch_shapes=[pltpu.VMEM((128, 128), F32)],
        compiler_params=params(2),
        name="scale",
    )(where, noise, conf_values, task_values, *pieces)


def back_kernel(where, task_basis, a, b, c, d, *refs):
    out, scaled = refs[-2:]
    x = where[1] // 4
    for far, ref in enumerate((a, b, c, d)):
        scaled[pl.ds(pl.multiple_of((x ^ far) * 32, 32), 32), :] = ref[...]
    kh, kl = split(mul3(scaled[...].T, task_basis[...], NT))
    out[:, 0:128] = kh
    out[:, 128:256] = kl


def rotate_back(where, task_basis, pieces, after):
    return pl.pallas_call(
        back_kernel,
        in_specs=scalars(1) + here(5) + anywhere(len(after)),
        out_specs=here(1)[0],
        out_shape=struct((512, 256), BF16),
        scratch_shapes=[pltpu.VMEM((128, 512), F32)],
        compiler_params=params(4),
        name="rotate_back",
    )(where, task_basis, *pieces, *after)


def expand_kernel(core, far, where, high, low, wide, *refs):
    for d in range(4):
        slot = d * 2 + core + far * 8
        rows = pl.ds(pl.multiple_of((where[0] ^ slot) * 256, 256), 256)
        both = mul(high[rows, :], wide[...])
        refs[-1][d] = both[:, :128] + (both[:, 128:] + mul(low[rows, :], wide[:, 0:128]))


def expand(core, far, where, high, low, wide, after):
    return pl.pallas_call(
        functools.partial(expand_kernel, core, far),
        in_specs=scalars(1) + here(3) + anywhere(len(after)),
        out_specs=here(1)[0],
        out_shape=struct((4, 256, 128)),
        compiler_params=params(14),
        cost_estimate=cost(1, 1),
        name="expand",
    )(where, high, low, wide, *after)


def pairs_kernel(mine, theirs, *outs):
    for d in range(4):
        outs[d][...] = mine[d] + theirs[d]


def sum_pairs(mine, theirs):
    return pl.pallas_call(
        pairs_kernel,
        in_specs=here(2),
        out_specs=here(4),
        out_shape=[struct((256, 128))] * 4,
        compiler_params=params(6),
        name="sum_over_core",
    )(mine, theirs)


def sum_kernel(count, copies, *refs):
    total = refs[0][...]
    for ref in refs[1:count]:
        total = total + ref[...]
    for ref in refs[-copies:]:
        ref[...] = total


def sum_blocks(blocks, after, copies=1):
    return pl.pallas_call(
        functools.partial(sum_kernel, len(blocks), copies),
        in_specs=here(len(blocks)) + anywhere(len(after)),
        out_specs=here(copies),
        out_shape=[struct((256, 128))] * copies,
        compiler_params=params(2),
        name="sum_over_y",
    )(*blocks, *after)


def row_digit(codes, k):
    part = (k >= 40).astype(jnp.int32) + (k >= 80).astype(jnp.int32) + (k >= 120).astype(jnp.int32)
    rest = k - 40 * part
    return part, rest & 3, lax.shift_right_logical(codes, 2 * lax.shift_right_logical(rest, 2)) & 3


def onehot_kernel(length_scales, codes, out, lengths):
    k = lax.broadcasted_iota(jnp.int32, (128, 128), 0)
    part, _, _ = row_digit(k, k)
    feature = lax.shift_right_logical(k - 40 * part, 2)
    value = jnp.zeros((128, 128), F32)
    for place in range(10):
        value = jnp.where(feature == place, length_scales[place] * (-1.0 / math.log(2.0)), value)
    lengths[...] = value

    for slot in range(16):
        row = codes[slot : slot + 1, :].astype(jnp.int32)
        _, level, digit = row_digit(jnp.broadcast_to(row, (128, 128)), k)
        hot = jnp.where(digit == level, 1.0, 0.0).astype(F32)
        out[slot * 128 : slot * 128 + 128, :] = hot.T.astype(BF16)


def onehot(length_scales, codes):
    return pl.pallas_call(
        onehot_kernel,
        in_specs=scalars(1) + here(1),
        out_specs=here(2),
        out_shape=[struct((2048, 128), BF16), struct((128, 128))],
        compiler_params=params(2),
        name="candidate_levels",
    )(length_scales, codes)


def cross_kernel(hot, codes0, codes1, lengths, high, low):
    k = lax.broadcasted_iota(jnp.int32, (128, 256), 0)
    length = jnp.concatenate([lengths[...], lengths[...]], axis=1)
    tables = []
    for codes in (codes0, codes1):
        row = codes[128:129, :].astype(jnp.int32)
        part, level, digit = row_digit(jnp.broadcast_to(row, (128, 256)), k)
        differ = (level - digit).astype(F32)
        value = length * differ * differ
        first = value.astype(BF16).astype(F32)
        second = (value - first).astype(BF16).astype(F32)
        third = value - first - second
        piece = jnp.where(part == 0, first, jnp.where(part == 1, second, jnp.where(part == 2, third, 0.0)))
        tables.append(piece.astype(BF16))
    table = jnp.concatenate(tables, axis=1)

    def step(i, carry):
        for part in range(4):
            rows = pl.ds(pl.multiple_of(i * (256 * 4) + part * 256, 256), 256)
            h, l = split(jnp.exp2(mul(hot[rows, :], table)))
            high[rows, :] = h
            low[rows, :] = l
        return carry

    lax.fori_loop(0, 8 // 4, step, 0)


def cross_halves(hot, block0, block1, lengths):
    return pl.pallas_call(
        cross_kernel,
        in_specs=here(4),
        out_specs=here(2),
        out_shape=[struct((2048, 512), BF16)] * 2,
        compiler_params=params(8),
        cost_estimate=cost(1, 1),
        name="cross",
    )(hot, block0, block1, lengths)


def predict_kernel(first, near0, near1, other0, other1, h0, l0, h1, l1, *refs):
    total, out, wide = (refs[0] if len(refs) == 3 else None), refs[-2], refs[-1]
    for place, ref in enumerate((near0, near1, other0, other1)):
        rows = pl.ds(place * 256, 256)
        wh, wl = split(ref[...])
        wide[rows, 0:128] = wh
        wide[rows, 128:256] = wl

    parts = min(4, out.shape[0] // 256)

    def step(i, carry):
        for part in range(parts):
            start = i * (256 * parts) + part * 256
            rows = pl.ds(pl.multiple_of(first + start, 256), 256)
            both = mul(h0[rows, :], wide[0:512, :]) + mul(h1[rows, :], wide[512:1024, :])
            rest = mul(l0[rows, :], wide[0:512, 0:128]) + mul(l1[rows, :], wide[512:1024, 0:128])
            value = both[:, :128] + (both[:, 128:] + rest)
            out[pl.ds(pl.multiple_of(start, 256), 256), :] = value if total is None else total[rows, :] + value
        return carry

    lax.fori_loop(0, out.shape[0] // (256 * parts), step, 0)


def predict(near, other, cross0, cross1, total, first, count):
    extra = [] if total is None else [total]
    return pl.pallas_call(
        functools.partial(predict_kernel, first),
        in_specs=here(8 + len(extra)),
        out_specs=here(1)[0],
        out_shape=struct((count, 128)),
        scratch_shapes=[pltpu.VMEM((1024, 256), BF16)],
        compiler_params=params(14),
        cost_estimate=cost(1, 1),
        name="predict",
    )(*near, *other, *cross0, *cross1, *extra)


def quarter_kernel(a, b, c, d, *outs):
    for g in range(4):
        rows = pl.ds(g * 128, 128)
        outs[g][...] = (a[rows, :] + b[rows, :]) + (c[rows, :] + d[rows, :])


def sum_quarters(blocks):
    return pl.pallas_call(
        quarter_kernel,
        in_specs=here(4),
        out_specs=here(4),
        out_shape=[struct((128, 128))] * 4,
        compiler_params=params(3),
        name="means_over_x",
    )(*blocks)


def finish_kernel(signal, a, b, c, d, task_basis, task_values, out):
    kernel = mul3(task_basis[...] * task_values[...], task_basis[...], NT)
    out[...] = signal[0] * mul3((a[...] + b[...]) + (c[...] + d[...]), kernel)


def finish(signal, parts, task_basis, task_values):
    return pl.pallas_call(
        finish_kernel,
        in_specs=scalars(1) + here(6),
        out_specs=here(1)[0],
        out_shape=struct((128, 128)),
        compiler_params=params(2),
        name="finish",
    )(signal, *parts, task_basis, task_values)


def local(
    basis,
    conf_values,
    task_basis,
    task_values,
    noise,
    observations,
    train_codes,
    length_scales,
    signal,
    cand_codes,
):
    n = lax.axis_index("narrow").astype(jnp.int32)
    w = lax.axis_index("wide").astype(jnp.int32)
    where = jnp.stack([n, w])

    own = own_block(where, observations, train_codes)
    high, low = halves(basis)
    mirror = gate(swap(own, "narrow", 8), [high])
    blocks = []
    for first in (own, mirror):
        near = [first] + [swap(first, "narrow", 2 * d) for d in (1, 2, 3)]
        blocks += near + [swap(block, "narrow", 1) for block in near]

    before = project_near(where, high, low, blocks[:8])
    pieces = project(where, high, low, task_basis, cand_codes[None], before, blocks[8:])
    mine = collect([pieces[0]] + [swap(pieces[d], "wide", 4 * d) for d in (1, 2, 3)])
    arrived = [mine] + [swap(mine, "wide", d) for d in (1, 2, 3)]
    scaled, codes = scale(where, noise, conf_values[None], task_values[None], arrived)
    quarters = [scaled] + [swap(scaled, "wide", 4 * d) for d in (1, 2, 3)]

    hot, lengths = onehot(length_scales, codes)
    crosses = {}
    for far in range(2):
        for pair in range(2):
            for core in range(2):
                first = far * 8 + core * 4 + pair * 2
                crosses[far, pair, core] = cross_halves(hot, blocks[first], blocks[first + 1], lengths)
    ready = [crosses[place][0] for place in crosses]

    wide = rotate_back(where, task_basis, quarters, ready[0:3])
    odd = expand(1, 1, where, high, low, wide, [])
    even = expand(0, 1, where, high, low, wide, [])
    sums = sum_pairs(even, swap(odd, "narrow", 1))
    odd = expand(1, 0, where, high, low, wide, [sums[0]])
    even = expand(0, 0, where, high, low, wide, [sums[0]])
    later = sum_pairs(even, swap(odd, "narrow", 1))
    total = [sums[0]] + [swap(sums[d], "narrow", 2 * d) for d in (1, 2, 3)]
    mirror = swap(sum_blocks(total, [later[0]] + ready[3:5])[0], "narrow", 8)
    total = [later[0]] + [swap(later[d], "narrow", 2 * d) for d in (1, 2, 3)]
    block, coefficients = sum_blocks(total + [mirror], ready[5:8], 2)

    means = None
    for far, first in enumerate((block, swap(block, "narrow", 8))):
        near = [first] + [swap(first, "narrow", 2 * d) for d in (1, 2, 3)]
        other, before = [], means
        for pair in range(2):
            if pair == 1:
                near[2:] = [gate(value, [before if far else means]) for value in near[2:]]
            other += [swap(value, "narrow", 1) for value in near[2 * pair : 2 * pair + 2]]
            group = near[2 * pair : 2 * pair + 2], other[2 * pair : 2 * pair + 2]
            group += crosses[far, pair, 0], crosses[far, pair, 1]
            if far + pair < 2:
                means = predict(*group, means, 0, 2048)
    last = {g: predict(*group, means, g * 512, 512) for g in (2, 1, 3, 0)}
    quarters = sum_quarters([last[0]] + [swap(last[g], "wide", 4 * g) for g in (2, 1, 3)])
    ends = [quarters[0]] + [swap(quarters[g], "wide", g) for g in (1, 2, 3)]
    return coefficients, finish(signal, ends, task_basis, task_values[None])


def solution(mesh):
    return jax.shard_map(
        local,
        mesh=mesh,
        in_specs=(
            P("wide", "narrow"),
            P("narrow"),
            P(),
            P(),
            P(),
            P(("wide", "narrow"), None),
            P(("wide", "narrow")),
            P(),
            P(),
            P("wide"),
        ),
        out_specs=(P(("wide", "narrow"), None), P(("wide", "narrow"), None)),
        check_vma=False,
    )
```

```python
import functools
import math

import jax
import jax.numpy as jnp
from jax import lax
from jax.experimental import pallas as pl
from jax.experimental.pallas import tpu as pltpu
from jax.sharding import PartitionSpec as P

F32 = jnp.float32
BF16 = jnp.bfloat16
VM = pltpu.VMEM
MIB = 1 << 20


def far_memory(value):
    return pltpu.with_memory_space_constraint(value, pltpu.HBM)


def split(x):
    high = x.astype(BF16)
    return high, (x - high.astype(F32)).astype(BF16)


def mul(a, b, dims=(((1,), (0,)), ((), ()))):
    return lax.dot_general(a, b, dims, preferred_element_type=F32)


def mul3(a, b, dims=(((1,), (0,)), ((), ()))):
    ah, al = split(a)
    bh, bl = split(b)
    return mul(ah, bh, dims) + (mul(ah, bl, dims) + mul(al, bh, dims))


NT = (((1,), (1,)), ((), ()))


def swap(value, axis, bits):
    return lax.ppermute(value, axis, [(i, i ^ bits) for i in range(16)])


def full(shape):
    return pl.BlockSpec(shape, lambda *_: (0,) * len(shape))


def params(mib):
    return pltpu.CompilerParams(vmem_limit_bytes=mib * MIB)


def here(count):
    return [pl.BlockSpec(memory_space=VM)] * count


def scalars(count):
    return [pl.BlockSpec(memory_space=pltpu.SMEM)] * count


def anywhere(count):
    return [pl.BlockSpec(memory_space=pl.ANY)] * count


def struct(shape, dtype=F32):
    return jax.ShapeDtypeStruct(shape, dtype)


def cost(flops=0, moved=0, transcendentals=0):
    return pl.CostEstimate(flops=flops, bytes_accessed=moved, transcendentals=transcendentals)


def halves_kernel(basis, high, low, held, arrived):
    def fetch(step):
        rows = pl.ds(pl.multiple_of(step * 512, 512), 512)
        return pltpu.make_async_copy(basis.at[rows, :], held.at[rows, :], arrived.at[step])

    for step in range(8):
        fetch(step).start()

    def part(step, carry):
        fetch(step).wait()
        rows = pl.ds(pl.multiple_of(step * 512, 512), 512)
        h, l = split(held[rows, :])
        high[rows, :] = h
        low[rows, :] = l
        return carry

    lax.fori_loop(0, 8, part, 0)


def halves(basis):
    return pl.pallas_call(
        halves_kernel,
        in_specs=anywhere(1),
        out_specs=here(2),
        out_shape=[struct((4096, 512), BF16)] * 2,
        scratch_shapes=[pltpu.VMEM((4096, 512), F32), pltpu.SemaphoreType.DMA((8,))],
        compiler_params=params(20),
        cost_estimate=cost(1, 1),
        name="basis_halves",
    )(far_memory(basis))


def stack_kernel(count, *refs):
    for place in range(count):
        refs[-1][place] = refs[place][...]


def stack(values, after):
    return pl.pallas_call(
        functools.partial(stack_kernel, len(values)),
        in_specs=here(len(values)) + anywhere(len(after)),
        out_specs=here(1)[0],
        out_shape=struct((len(values), *values[0].shape)),
        compiler_params=params(3),
        name="stack",
    )(*values, *after)


def own_kernel(where, observations, codes, out):
    out[0:128, :] = observations[...].T
    out[128:136, :] = jnp.broadcast_to(codes[...].astype(F32), (8, 256))


def own_block(where, observations, codes):
    return pl.pallas_call(
        own_kernel,
        grid=(1,),
        in_specs=scalars(1) + [full((256, 128)), full((1, 256))],
        out_specs=full((136, 256)),
        out_shape=struct((136, 256)),
        compiler_params=params(2),
        name="own_observations",
    )(where, far_memory(observations), far_memory(codes[None]))


def project_part(me, high, low, total, near, other, first, far):
    def step(i, total):
        for part in range(2):
            for core, ref in enumerate((near, other)):
                slot = (first + i * 2 + part) * 2 + core + far * 8
                rows = pl.ds(pl.multiple_of((me ^ slot) * 256, 256), 256)
                oh, ol = split(ref[i * 2 + part, 0:128, :])
                both = mul(jnp.concatenate([oh, ol], axis=0), high[rows, :])
                total = total + both[:128] + (both[128:] + mul(oh, low[rows, :]))
        return total

    return lax.fori_loop(0, near.shape[0] // 2, step, total)


def near_kernel(where, high, low, near, other, out):
    out[...] = project_part(where[0], high, low, jnp.zeros((128, 512), F32), near, other, 0, 0)


def project_near(where, high, low, near, other):
    return pl.pallas_call(
        near_kernel,
        in_specs=scalars(1) + here(4),
        out_specs=here(1)[0],
        out_shape=struct((128, 512)),
        compiler_params=params(16),
        cost_estimate=cost(1, 1),
        name="project_near",
    )(where, high, low, near, other)


def project_kernel(where, high, low, task_basis, cand, before, near0, other0, near1, other1, *refs):
    outs, rotated = refs[:4], refs[4]
    me, x = where[0], where[1] // 4
    total = project_part(me, high, low, before[...], near0, other0, 0, 1)
    total = project_part(me, high, low, total, near1, other1, 2, 1)
    rotated[...] = mul3(task_basis[...].T, total)
    columns = pl.ds(pl.multiple_of(me * 128, 128), 128)
    codes = jnp.broadcast_to(cand[:, columns].astype(F32), (8, 128))
    for d in range(4):
        outs[d][0:32, :] = rotated[pl.ds(pl.multiple_of((x ^ d) * 32, 32), 32), :]
        outs[d][32:40, :] = jnp.concatenate([codes] * 4, axis=1)


def project(where, high, low, task_basis, cand, before, pairs):
    return pl.pallas_call(
        project_kernel,
        in_specs=scalars(1) + here(9),
        out_specs=here(4),
        out_shape=[struct((40, 512))] * 4,
        scratch_shapes=[pltpu.VMEM((128, 512), F32)],
        compiler_params=params(16),
        cost_estimate=cost(1, 1),
        name="project",
    )(where, high, low, task_basis, cand, before, *pairs)


def collect_kernel(own, a, b, c, out):
    out[0:32, :] = (own[0:32, :] + a[0:32, :]) + (b[0:32, :] + c[0:32, :])
    rows = [ref[32:33, :] for ref in (own, a, b, c)]
    out[32:40, :] = jnp.concatenate(rows + rows, axis=0)


def collect(pieces):
    return pl.pallas_call(
        collect_kernel,
        in_specs=here(4),
        out_specs=here(1)[0],
        out_shape=struct((40, 512)),
        compiler_params=params(2),
        name="sum_over_x",
    )(*pieces)


def scale_kernel(where, noise, conf_values, task_values, own, a, b, c, out, codes, column):
    column[...] = jnp.broadcast_to(task_values[...], (128, 128)).T
    rows = pl.ds(pl.multiple_of(where[1] // 4 * 32, 32), 32)
    total = (own[0:32, :] + a[0:32, :]) + (b[0:32, :] + c[0:32, :])
    out[...] = total / (conf_values[...] * column[rows, 0:1] + noise[0])
    for far in range(4):
        for near, ref in enumerate((own, a, b, c)):
            slot = far * 4 + near
            codes[slot : slot + 1, :] = ref[32 + far : 33 + far, 0:128]


def scale(where, noise, conf_values, task_values, pieces):
    return pl.pallas_call(
        scale_kernel,
        in_specs=scalars(2) + here(6),
        out_specs=here(2),
        out_shape=[struct((32, 512)), struct((16, 128))],
        scratch_shapes=[pltpu.VMEM((128, 128), F32)],
        compiler_params=params(2),
        name="scale",
    )(where, noise, conf_values, task_values, *pieces)


def back_kernel(where, task_basis, a, b, c, d, *refs):
    out, scaled = refs[-2:]
    x = where[1] // 4
    for far, ref in enumerate((a, b, c, d)):
        scaled[pl.ds(pl.multiple_of((x ^ far) * 32, 32), 32), :] = ref[...]
    kh, kl = split(mul3(scaled[...].T, task_basis[...], NT))
    out[:, 0:128] = kh
    out[:, 128:256] = kl


def rotate_back(where, task_basis, pieces, after):
    return pl.pallas_call(
        back_kernel,
        in_specs=scalars(1) + here(5) + anywhere(len(after)),
        out_specs=here(1)[0],
        out_shape=struct((512, 256), BF16),
        scratch_shapes=[pltpu.VMEM((128, 512), F32)],
        compiler_params=params(4),
        name="rotate_back",
    )(where, task_basis, *pieces, *after)


def expand_kernel(core, far, where, high, low, wide, *refs):
    def step(i, carry):
        for d in (i * 2, i * 2 + 1):
            slot = d * 2 + core + far * 8
            rows = pl.ds(pl.multiple_of((where[0] ^ slot) * 256, 256), 256)
            both = mul(high[rows, :], wide[...])
            refs[-1][d] = both[:, :128] + (both[:, 128:] + mul(low[rows, :], wide[:, 0:128]))
        return carry

    lax.fori_loop(0, 2, step, 0)


def expand(core, far, where, high, low, wide, after):
    return pl.pallas_call(
        functools.partial(expand_kernel, core, far),
        in_specs=scalars(1) + here(3) + anywhere(len(after)),
        out_specs=here(1)[0],
        out_shape=struct((4, 256, 128)),
        compiler_params=params(14),
        cost_estimate=cost(1, 1),
        name="expand",
    )(where, high, low, wide, *after)


def pairs_kernel(mine, theirs, *outs):
    for d in range(4):
        outs[d][...] = mine[d] + theirs[d]


def sum_pairs(mine, theirs):
    return pl.pallas_call(
        pairs_kernel,
        in_specs=here(2),
        out_specs=here(4),
        out_shape=[struct((256, 128))] * 4,
        compiler_params=params(6),
        name="sum_over_core",
    )(mine, theirs)


def sum_kernel(count, copies, *refs):
    total = refs[0][...]
    for ref in refs[1:count]:
        total = total + ref[...]
    for ref in refs[-copies:]:
        ref[...] = total


def sum_blocks(blocks, after, copies=1):
    return pl.pallas_call(
        functools.partial(sum_kernel, len(blocks), copies),
        in_specs=here(len(blocks)) + anywhere(len(after)),
        out_specs=here(copies),
        out_shape=[struct((256, 128))] * copies,
        compiler_params=params(2),
        name="sum_over_y",
    )(*blocks, *after)


def row_digit(codes, k):
    part = (k >= 40).astype(jnp.int32) + (k >= 80).astype(jnp.int32) + (k >= 120).astype(jnp.int32)
    rest = k - 40 * part
    return part, rest & 3, lax.shift_right_logical(codes, 2 * lax.shift_right_logical(rest, 2)) & 3


def onehot_kernel(length_scales, codes, out, lengths):
    k = lax.broadcasted_iota(jnp.int32, (128, 128), 0)
    part, _, _ = row_digit(k, k)
    feature = lax.shift_right_logical(k - 40 * part, 2)
    value = jnp.zeros((128, 128), F32)
    for place in range(10):
        value = jnp.where(feature == place, length_scales[place] * (-1.0 / math.log(2.0)), value)
    lengths[...] = value

    for slot in range(16):
        row = codes[slot : slot + 1, :].astype(jnp.int32)
        _, level, digit = row_digit(jnp.broadcast_to(row, (128, 128)), k)
        hot = jnp.where(digit == level, 1.0, 0.0).astype(F32)
        out[slot * 128 : slot * 128 + 128, :] = hot.T.astype(BF16)


def onehot(length_scales, codes):
    return pl.pallas_call(
        onehot_kernel,
        in_specs=scalars(1) + here(1),
        out_specs=here(2),
        out_shape=[struct((2048, 128), BF16), struct((128, 128))],
        compiler_params=params(2),
        name="candidate_levels",
    )(length_scales, codes)


def cross_kernel(firsts, hot, lengths, *refs):
    count = len(firsts)
    outs, table = refs[-1 - 2 * count : -1], refs[-1]
    k = lax.broadcasted_iota(jnp.int32, (128, 256), 0)
    length = jnp.concatenate([lengths[...], lengths[...]], axis=1)
    for place, first in enumerate(firsts):
        for part in range(2):
            row = refs[place][first + part, 128:129, :].astype(jnp.int32)
            piece, level, digit = row_digit(jnp.broadcast_to(row, (128, 256)), k)
            differ = (level - digit).astype(F32)
            value = length * differ * differ
            one = value.astype(BF16).astype(F32)
            two = (value - one).astype(BF16).astype(F32)
            three = value - one - two
            value = jnp.where(piece == 0, one, jnp.where(piece == 1, two, jnp.where(piece == 2, three, 0.0)))
            table[:, part * 256 : part * 256 + 256] = value.astype(BF16)

        def step(i, carry, high=outs[2 * place], low=outs[2 * place + 1]):
            for part in range(2):
                rows = pl.ds(pl.multiple_of(i * (256 * 2) + part * 256, 256), 256)
                h, l = split(jnp.exp2(mul(hot[rows, :], table[...])))
                high[rows, :] = h
                low[rows, :] = l
            return carry

        lax.fori_loop(0, 8 // 2, step, 0)


def cross_halves(hot, lengths, sources, after):
    arrays, firsts = zip(*sources)
    count = len(sources)
    outs = pl.pallas_call(
        functools.partial(cross_kernel, firsts),
        in_specs=here(2 + count) + anywhere(len(after)),
        out_specs=here(2 * count),
        out_shape=[struct((2048, 512), BF16)] * (2 * count),
        scratch_shapes=[pltpu.VMEM((128, 512), BF16)],
        compiler_params=params(16),
        cost_estimate=cost(1, 1),
        name="cross",
    )(hot, lengths, *arrays, *after)
    return [tuple(outs[2 * place : 2 * place + 2]) for place in range(count)]


def predict_kernel(first, near_first, has_total, near, other, h0, l0, h1, l1, *refs):
    total, out, wide = (refs[0] if has_total else None), refs[-2], refs[-1]
    for core, ref in enumerate((near, other)):
        for part in range(2):
            rows = pl.ds(core * 512 + part * 256, 256)
            wh, wl = split(ref[near_first + part])
            wide[rows, 0:128] = wh
            wide[rows, 128:256] = wl

    def step(i, carry):
        for part in range(2):
            start = i * 512 + part * 256
            rows = pl.ds(pl.multiple_of(first + start, 256), 256)
            both = mul(h0[rows, :], wide[0:512, :]) + mul(h1[rows, :], wide[512:1024, :])
            rest = mul(l0[rows, :], wide[0:512, 0:128]) + mul(l1[rows, :], wide[512:1024, 0:128])
            value = both[:, :128] + (both[:, 128:] + rest)
            out[pl.ds(pl.multiple_of(start, 256), 256), :] = value if total is None else total[rows, :] + value
        return carry

    lax.fori_loop(0, out.shape[0] // 512, step, 0)


def predict(near, other, near_first, cross0, cross1, total, first, count, after=()):
    extra = [] if total is None else [total]
    return pl.pallas_call(
        functools.partial(predict_kernel, first, near_first, total is not None),
        in_specs=here(6 + len(extra)) + anywhere(len(after)),
        out_specs=here(1)[0],
        out_shape=struct((count, 128)),
        scratch_shapes=[pltpu.VMEM((1024, 256), BF16)],
        compiler_params=params(14),
        cost_estimate=cost(1, 1),
        name="predict",
    )(near, other, *cross0, *cross1, *extra, *after)


def quarter_kernel(a, b, c, d, *outs):
    for g in range(4):
        rows = pl.ds(g * 128, 128)
        outs[g][...] = (a[rows, :] + b[rows, :]) + (c[rows, :] + d[rows, :])


def sum_quarters(blocks):
    return pl.pallas_call(
        quarter_kernel,
        in_specs=here(4),
        out_specs=here(4),
        out_shape=[struct((128, 128))] * 4,
        compiler_params=params(3),
        name="means_over_x",
    )(*blocks)


def finish_kernel(signal, a, b, c, d, task_basis, task_values, out):
    kernel = mul3(task_basis[...] * task_values[...], task_basis[...], NT)
    out[...] = signal[0] * mul3((a[...] + b[...]) + (c[...] + d[...]), kernel)


def finish(signal, parts, task_basis, task_values):
    return pl.pallas_call(
        finish_kernel,
        in_specs=scalars(1) + here(6),
        out_specs=here(1)[0],
        out_shape=struct((128, 128)),
        compiler_params=params(2),
        name="finish",
    )(signal, *parts, task_basis, task_values)


def local(
    basis,
    conf_values,
    task_basis,
    task_values,
    noise,
    observations,
    train_codes,
    length_scales,
    signal,
    cand_codes,
):
    n = lax.axis_index("narrow").astype(jnp.int32)
    w = lax.axis_index("wide").astype(jnp.int32)
    where = jnp.stack([n, w])

    own = own_block(where, observations, train_codes)
    high, low = halves(basis)
    near = stack([own] + [swap(own, "narrow", 2 * d) for d in (1, 2, 3)], [high])
    other = swap(near, "narrow", 1)
    before = project_near(where, high, low, near, other)
    mirror = swap(own, "narrow", 8)
    far = [mirror] + [swap(mirror, "narrow", 2 * d) for d in (1, 2, 3)]
    pairs = []
    for pair in (stack(far[:2], []), stack(far[2:], [])):
        pairs += [pair, swap(pair, "narrow", 1)]
    pieces = project(where, high, low, task_basis, cand_codes[None], before, pairs)
    mine = collect([pieces[0]] + [swap(pieces[d], "wide", 4 * d) for d in (1, 2, 3)])
    arrived = [mine] + [swap(mine, "wide", d) for d in (1, 2, 3)]
    scaled, codes = scale(where, noise, conf_values[None], task_values[None], arrived)
    quarters = [scaled] + [swap(scaled, "wide", 4 * d) for d in (1, 2, 3)]

    hot, lengths = onehot(length_scales, codes)
    sources = [(near, 0), (other, 0), (near, 2), (other, 2)] + [(array, 0) for array in pairs]
    crosses = cross_halves(hot, lengths, sources[:3], [])
    wide = rotate_back(where, task_basis, quarters, [crosses[0][0]])
    odd = expand(1, 1, where, high, low, wide, [])
    even = expand(0, 1, where, high, low, wide, [])
    sums = sum_pairs(even, swap(odd, "narrow", 1))
    odd = expand(1, 0, where, high, low, wide, [sums[0]])
    even = expand(0, 0, where, high, low, wide, [sums[0]])
    later = sum_pairs(even, swap(odd, "narrow", 1))
    total = [sums[0]] + [swap(sums[d], "narrow", 2 * d) for d in (1, 2, 3)]
    total = sum_blocks(total, [later[0]])[0]
    mirror = swap(total, "narrow", 8)
    crosses += cross_halves(hot, lengths, sources[3:6], [total])
    total = [later[0]] + [swap(later[d], "narrow", 2 * d) for d in (1, 2, 3)]
    block, coefficients = sum_blocks(total + [mirror], [crosses[5][0]], 2)

    mirror = swap(block, "narrow", 8)
    crosses += cross_halves(hot, lengths, sources[6:], [block])
    near = stack([block] + [swap(block, "narrow", 2 * d) for d in (1, 2, 3)], [mirror, crosses[6][0]])
    other = swap(near, "narrow", 1)
    start = predict(near, other, 0, *crosses[0:2], None, 0, 2048)
    means = predict(near, other, 2, *crosses[2:4], start, 0, 2048)
    far = [mirror] + [swap(mirror, "narrow", 2 * d) for d in (1, 2, 3)]
    near = stack(far[:2], [start])
    other = swap(near, "narrow", 1)
    after = [means]
    means = predict(near, other, 0, *crosses[4:6], means, 0, 2048)
    near = stack(far[2:], after)
    other = swap(near, "narrow", 1)
    last, after = {}, []
    for g in (2, 1, 3, 0):
        last[g] = predict(near, other, 0, *crosses[6:8], means, g * 512, 512, after)
        after = [last[g]]
    quarters = sum_quarters([last[0]] + [swap(last[g], "wide", 4 * g) for g in (2, 1, 3)])
    ends = [quarters[0]] + [swap(quarters[g], "wide", g) for g in (1, 2, 3)]
    return coefficients, finish(signal, ends, task_basis, task_values[None])


def solution(mesh):
    return jax.shard_map(
        local,
        mesh=mesh,
        in_specs=(
            P("wide", "narrow"),
            P("narrow"),
            P(),
            P(),
            P(),
            P(("wide", "narrow"), None),
            P(("wide", "narrow")),
            P(),
            P(),
            P("wide"),
        ),
        out_specs=(P(("wide", "narrow"), None), P(("wide", "narrow"), None)),
        check_vma=False,
    )
```

```python
import functools
import math

import jax
import jax.numpy as jnp
from jax import lax
from jax.experimental import pallas as pl
from jax.experimental.pallas import tpu as pltpu
from jax.sharding import PartitionSpec as P

F32 = jnp.float32
BF16 = jnp.bfloat16
VM = pltpu.VMEM
MIB = 1 << 20


def far_memory(value):
    return pltpu.with_memory_space_constraint(value, pltpu.HBM)


def split(x):
    high = x.astype(BF16)
    return high, (x - high.astype(F32)).astype(BF16)


def mul(a, b, dims=(((1,), (0,)), ((), ()))):
    return lax.dot_general(a, b, dims, preferred_element_type=F32)


def mul3(a, b, dims=(((1,), (0,)), ((), ()))):
    ah, al = split(a)
    bh, bl = split(b)
    return mul(ah, bh, dims) + (mul(ah, bl, dims) + mul(al, bh, dims))


NT = (((1,), (1,)), ((), ()))


def swap(value, axis, bits):
    return lax.ppermute(value, axis, [(i, i ^ bits) for i in range(16)])


def full(shape):
    return pl.BlockSpec(shape, lambda *_: (0,) * len(shape))


def params(mib):
    return pltpu.CompilerParams(vmem_limit_bytes=mib * MIB)


def here(count):
    return [pl.BlockSpec(memory_space=VM)] * count


def scalars(count):
    return [pl.BlockSpec(memory_space=pltpu.SMEM)] * count


def anywhere(count):
    return [pl.BlockSpec(memory_space=pl.ANY)] * count


def struct(shape, dtype=F32):
    return jax.ShapeDtypeStruct(shape, dtype)


def cost(flops=0, moved=0, transcendentals=0):
    return pl.CostEstimate(flops=flops, bytes_accessed=moved, transcendentals=transcendentals)


def halves_kernel(basis, high, low, held, arrived):
    def fetch(step):
        rows = pl.ds(pl.multiple_of(step * 512, 512), 512)
        return pltpu.make_async_copy(basis.at[rows, :], held.at[rows, :], arrived.at[step])

    for step in range(8):
        fetch(step).start()

    def part(step, carry):
        fetch(step).wait()
        rows = pl.ds(pl.multiple_of(step * 512, 512), 512)
        h, l = split(held[rows, :])
        high[rows, :] = h
        low[rows, :] = l
        return carry

    lax.fori_loop(0, 8, part, 0)


def halves(basis):
    return pl.pallas_call(
        halves_kernel,
        in_specs=anywhere(1),
        out_specs=here(2),
        out_shape=[struct((4096, 512), BF16)] * 2,
        scratch_shapes=[pltpu.VMEM((4096, 512), F32), pltpu.SemaphoreType.DMA((8,))],
        compiler_params=params(20),
        cost_estimate=cost(1, 1),
        name="basis_halves",
    )(far_memory(basis))


def stack_kernel(count, *refs):
    for place in range(count):
        refs[-1][place] = refs[place][...]


def stack(values, after):
    return pl.pallas_call(
        functools.partial(stack_kernel, len(values)),
        in_specs=here(len(values)) + anywhere(len(after)),
        out_specs=here(1)[0],
        out_shape=struct((len(values), *values[0].shape)),
        compiler_params=params(3),
        name="stack",
    )(*values, *after)


def own_kernel(where, observations, codes, out):
    out[0:128, :] = observations[...].T
    out[128:136, :] = jnp.broadcast_to(codes[...].astype(F32), (8, 256))


def own_block(where, observations, codes):
    return pl.pallas_call(
        own_kernel,
        grid=(1,),
        in_specs=scalars(1) + [full((256, 128)), full((1, 256))],
        out_specs=full((136, 256)),
        out_shape=struct((136, 256)),
        compiler_params=params(2),
        name="own_observations",
    )(where, far_memory(observations), far_memory(codes[None]))


def project_part(me, high, low, total, near, other, first, far):
    def step(i, total):
        for part in range(2):
            for core, ref in enumerate((near, other)):
                slot = (first + i * 2 + part) * 2 + core + far * 8
                rows = pl.ds(pl.multiple_of((me ^ slot) * 256, 256), 256)
                oh, ol = split(ref[i * 2 + part, 0:128, :])
                both = mul(jnp.concatenate([oh, ol], axis=0), high[rows, :])
                total = total + both[:128] + (both[128:] + mul(oh, low[rows, :]))
        return total

    return lax.fori_loop(0, near.shape[0] // 2, step, total)


def near_kernel(where, high, low, near, other, out):
    out[...] = project_part(where[0], high, low, jnp.zeros((128, 512), F32), near, other, 0, 0)


def project_near(where, high, low, near, other):
    return pl.pallas_call(
        near_kernel,
        in_specs=scalars(1) + here(4),
        out_specs=here(1)[0],
        out_shape=struct((128, 512)),
        compiler_params=params(16),
        cost_estimate=cost(1, 1),
        name="project_near",
    )(where, high, low, near, other)


def project_kernel(where, high, low, task_basis, cand, before, near0, other0, near1, other1, *refs):
    outs, rotated = refs[:4], refs[4]
    me, x = where[0], where[1] // 4
    total = project_part(me, high, low, before[...], near0, other0, 0, 1)
    total = project_part(me, high, low, total, near1, other1, 2, 1)
    rotated[...] = mul3(task_basis[...].T, total)
    columns = pl.ds(pl.multiple_of(me * 128, 128), 128)
    codes = jnp.broadcast_to(cand[:, columns].astype(F32), (8, 128))
    for d in range(4):
        outs[d][0:32, :] = rotated[pl.ds(pl.multiple_of((x ^ d) * 32, 32), 32), :]
        outs[d][32:40, :] = jnp.concatenate([codes] * 4, axis=1)


def project(where, high, low, task_basis, cand, before, pairs):
    return pl.pallas_call(
        project_kernel,
        in_specs=scalars(1) + here(9),
        out_specs=here(4),
        out_shape=[struct((40, 512))] * 4,
        scratch_shapes=[pltpu.VMEM((128, 512), F32)],
        compiler_params=params(16),
        cost_estimate=cost(1, 1),
        name="project",
    )(where, high, low, task_basis, cand, before, *pairs)


def collect_kernel(own, a, b, c, out):
    out[0:32, :] = (own[0:32, :] + a[0:32, :]) + (b[0:32, :] + c[0:32, :])
    rows = [ref[32:33, :] for ref in (own, a, b, c)]
    out[32:40, :] = jnp.concatenate(rows + rows, axis=0)


def collect(pieces):
    return pl.pallas_call(
        collect_kernel,
        in_specs=here(4),
        out_specs=here(1)[0],
        out_shape=struct((40, 512)),
        compiler_params=params(2),
        name="sum_over_x",
    )(*pieces)


def scale_kernel(where, noise, conf_values, task_values, own, a, b, c, out, codes, column):
    column[...] = jnp.broadcast_to(task_values[...], (128, 128)).T
    rows = pl.ds(pl.multiple_of(where[1] // 4 * 32, 32), 32)
    total = (own[0:32, :] + a[0:32, :]) + (b[0:32, :] + c[0:32, :])
    out[...] = total / (conf_values[...] * column[rows, 0:1] + noise[0])
    for far in range(4):
        for near, ref in enumerate((own, a, b, c)):
            slot = far * 4 + near
            codes[slot : slot + 1, :] = ref[32 + far : 33 + far, 0:128]


def scale(where, noise, conf_values, task_values, pieces):
    return pl.pallas_call(
        scale_kernel,
        in_specs=scalars(2) + here(6),
        out_specs=here(2),
        out_shape=[struct((32, 512)), struct((16, 128))],
        scratch_shapes=[pltpu.VMEM((128, 128), F32)],
        compiler_params=params(2),
        name="scale",
    )(where, noise, conf_values, task_values, *pieces)


def back_kernel(where, task_basis, a, b, c, d, *refs):
    out, scaled = refs[-2:]
    x = where[1] // 4
    for far, ref in enumerate((a, b, c, d)):
        scaled[pl.ds(pl.multiple_of((x ^ far) * 32, 32), 32), :] = ref[...]
    kh, kl = split(mul3(scaled[...].T, task_basis[...], NT))
    out[:, 0:128] = kh
    out[:, 128:256] = kl


def rotate_back(where, task_basis, pieces, after):
    return pl.pallas_call(
        back_kernel,
        in_specs=scalars(1) + here(5) + anywhere(len(after)),
        out_specs=here(1)[0],
        out_shape=struct((512, 256), BF16),
        scratch_shapes=[pltpu.VMEM((128, 512), F32)],
        compiler_params=params(4),
        name="rotate_back",
    )(where, task_basis, *pieces, *after)


def expand_kernel(core, far, where, high, low, wide, *refs):
    def step(i, carry):
        for d in (i * 2, i * 2 + 1):
            slot = d * 2 + core + far * 8
            rows = pl.ds(pl.multiple_of((where[0] ^ slot) * 256, 256), 256)
            both = mul(high[rows, :], wide[...])
            refs[-1][d] = both[:, :128] + (both[:, 128:] + mul(low[rows, :], wide[:, 0:128]))
        return carry

    lax.fori_loop(0, 2, step, 0)


def expand(core, far, where, high, low, wide, after):
    return pl.pallas_call(
        functools.partial(expand_kernel, core, far),
        in_specs=scalars(1) + here(3) + anywhere(len(after)),
        out_specs=here(1)[0],
        out_shape=struct((4, 256, 128)),
        compiler_params=params(14),
        cost_estimate=cost(1, 1),
        name="expand",
    )(where, high, low, wide, *after)


def pairs_kernel(mine, theirs, *outs):
    for d in range(4):
        outs[d][...] = mine[d] + theirs[d]


def sum_pairs(mine, theirs):
    return pl.pallas_call(
        pairs_kernel,
        in_specs=here(2),
        out_specs=here(4),
        out_shape=[struct((256, 128))] * 4,
        compiler_params=params(6),
        name="sum_over_core",
    )(mine, theirs)


def sum_kernel(count, copies, *refs):
    total = refs[0][...]
    for ref in refs[1:count]:
        total = total + ref[...]
    for ref in refs[-copies:]:
        ref[...] = total


def sum_blocks(blocks, after, copies=1):
    return pl.pallas_call(
        functools.partial(sum_kernel, len(blocks), copies),
        in_specs=here(len(blocks)) + anywhere(len(after)),
        out_specs=here(copies),
        out_shape=[struct((256, 128))] * copies,
        compiler_params=params(2),
        name="sum_over_y",
    )(*blocks, *after)


def row_digit(codes, k):
    part = (k >= 40).astype(jnp.int32) + (k >= 80).astype(jnp.int32) + (k >= 120).astype(jnp.int32)
    rest = k - 40 * part
    return part, rest & 3, lax.shift_right_logical(codes, 2 * lax.shift_right_logical(rest, 2)) & 3


def onehot_kernel(length_scales, codes, out, lengths):
    k = lax.broadcasted_iota(jnp.int32, (128, 128), 0)
    part, _, _ = row_digit(k, k)
    feature = lax.shift_right_logical(k - 40 * part, 2)
    value = jnp.zeros((128, 128), F32)
    for place in range(10):
        value = jnp.where(feature == place, length_scales[place] * (-1.0 / math.log(2.0)), value)
    lengths[...] = value

    for slot in range(16):
        row = codes[slot : slot + 1, :].astype(jnp.int32)
        _, level, digit = row_digit(jnp.broadcast_to(row, (128, 128)), k)
        hot = jnp.where(digit == level, 1.0, 0.0).astype(F32)
        out[slot * 128 : slot * 128 + 128, :] = hot.T.astype(BF16)


def onehot(length_scales, codes):
    return pl.pallas_call(
        onehot_kernel,
        in_specs=scalars(1) + here(1),
        out_specs=here(2),
        out_shape=[struct((2048, 128), BF16), struct((128, 128))],
        compiler_params=params(2),
        name="candidate_levels",
    )(length_scales, codes)


def cross_kernel(firsts, hot, lengths, *refs):
    count = len(firsts)
    outs, table = refs[-1 - 2 * count : -1], refs[-1]
    k = lax.broadcasted_iota(jnp.int32, (128, 256), 0)
    length = jnp.concatenate([lengths[...], lengths[...]], axis=1)
    for place, first in enumerate(firsts):
        for part in range(2):
            row = refs[place][first + part, 128:129, :].astype(jnp.int32)
            piece, level, digit = row_digit(jnp.broadcast_to(row, (128, 256)), k)
            differ = (level - digit).astype(F32)
            value = length * differ * differ
            one = value.astype(BF16).astype(F32)
            two = (value - one).astype(BF16).astype(F32)
            three = value - one - two
            value = jnp.where(piece == 0, one, jnp.where(piece == 1, two, jnp.where(piece == 2, three, 0.0)))
            table[:, part * 256 : part * 256 + 256] = value.astype(BF16)

        def step(i, carry, high=outs[2 * place], low=outs[2 * place + 1]):
            for part in range(2):
                rows = pl.ds(pl.multiple_of(i * (256 * 2) + part * 256, 256), 256)
                h, l = split(jnp.exp2(mul(hot[rows, :], table[...])))
                high[rows, :] = h
                low[rows, :] = l
            return carry

        lax.fori_loop(0, 8 // 2, step, 0)


def cross_halves(hot, lengths, sources, after):
    arrays, firsts = zip(*sources)
    count = len(sources)
    outs = pl.pallas_call(
        functools.partial(cross_kernel, firsts),
        in_specs=here(2 + count) + anywhere(len(after)),
        out_specs=here(2 * count),
        out_shape=[struct((2048, 512), BF16)] * (2 * count),
        scratch_shapes=[pltpu.VMEM((128, 512), BF16)],
        compiler_params=params(16),
        cost_estimate=cost(1, 1),
        name="cross",
    )(hot, lengths, *arrays, *after)
    return [tuple(outs[2 * place : 2 * place + 2]) for place in range(count)]


def predict_kernel(first, near_first, has_total, near, other, h0, l0, h1, l1, *refs):
    total, out, wide = (refs[0] if has_total else None), refs[-2], refs[-1]
    for core, ref in enumerate((near, other)):
        for part in range(2):
            rows = pl.ds(core * 512 + part * 256, 256)
            wh, wl = split(ref[near_first + part])
            wide[rows, 0:128] = wh
            wide[rows, 128:256] = wl

    def step(i, carry):
        for part in range(2):
            start = i * 512 + part * 256
            rows = pl.ds(pl.multiple_of(first + start, 256), 256)
            both = mul(h0[rows, :], wide[0:512, :]) + mul(h1[rows, :], wide[512:1024, :])
            rest = mul(l0[rows, :], wide[0:512, 0:128]) + mul(l1[rows, :], wide[512:1024, 0:128])
            value = both[:, :128] + (both[:, 128:] + rest)
            out[pl.ds(pl.multiple_of(start, 256), 256), :] = value if total is None else total[rows, :] + value
        return carry

    lax.fori_loop(0, out.shape[0] // 512, step, 0)


def predict(near, other, near_first, cross0, cross1, total, first, count, after=()):
    extra = [] if total is None else [total]
    return pl.pallas_call(
        functools.partial(predict_kernel, first, near_first, total is not None),
        in_specs=here(6 + len(extra)) + anywhere(len(after)),
        out_specs=here(1)[0],
        out_shape=struct((count, 128)),
        scratch_shapes=[pltpu.VMEM((1024, 256), BF16)],
        compiler_params=params(14),
        cost_estimate=cost(1, 1),
        name="predict",
    )(near, other, *cross0, *cross1, *extra, *after)


def two_kernel(a, b, out):
    out[...] = a[...] + b[...]


def sum_two(a, b):
    return pl.pallas_call(
        two_kernel,
        in_specs=here(2),
        out_specs=here(1)[0],
        out_shape=struct(a.shape),
        compiler_params=params(3),
        name="sum_two",
    )(a, b)


def quarter_kernel(a, b, c, *outs):
    for g in range(4):
        rows = pl.ds(g * 128, 128)
        outs[g][...] = a[rows, :] + (b[rows, :] + c[rows, :])


def sum_quarters(blocks):
    return pl.pallas_call(
        quarter_kernel,
        in_specs=here(3),
        out_specs=here(4),
        out_shape=[struct((128, 128))] * 4,
        compiler_params=params(3),
        name="means_over_x",
    )(*blocks)


def finish_kernel(signal, a, b, c, d, task_basis, task_values, out):
    kernel = mul3(task_basis[...] * task_values[...], task_basis[...], NT)
    out[...] = signal[0] * mul3((a[...] + b[...]) + (c[...] + d[...]), kernel)


def finish(signal, parts, task_basis, task_values):
    return pl.pallas_call(
        finish_kernel,
        in_specs=scalars(1) + here(6),
        out_specs=here(1)[0],
        out_shape=struct((128, 128)),
        compiler_params=params(2),
        name="finish",
    )(signal, *parts, task_basis, task_values)


def local(
    basis,
    conf_values,
    task_basis,
    task_values,
    noise,
    observations,
    train_codes,
    length_scales,
    signal,
    cand_codes,
):
    n = lax.axis_index("narrow").astype(jnp.int32)
    w = lax.axis_index("wide").astype(jnp.int32)
    where = jnp.stack([n, w])

    own = own_block(where, observations, train_codes)
    high, low = halves(basis)
    mirror = swap(own, "narrow", 8)
    near = stack([own] + [swap(own, "narrow", 2 * d) for d in (1, 2, 3)], [high, mirror])
    other = swap(near, "narrow", 1)
    before = project_near(where, high, low, near, other)
    far = [mirror] + [swap(mirror, "narrow", 2 * d) for d in (1, 2, 3)]
    pairs = []
    for pair in (stack(far[:2], []), stack(far[2:], [])):
        pairs += [pair, swap(pair, "narrow", 1)]
    pieces = project(where, high, low, task_basis, cand_codes[None], before, pairs)
    mine = collect([pieces[0]] + [swap(pieces[d], "wide", 4 * d) for d in (1, 2, 3)])
    arrived = [mine] + [swap(mine, "wide", d) for d in (1, 2, 3)]
    scaled, codes = scale(where, noise, conf_values[None], task_values[None], arrived)
    quarters = [scaled] + [swap(scaled, "wide", 4 * d) for d in (1, 2, 3)]

    hot, lengths = onehot(length_scales, codes)
    sources = [(near, 0), (other, 0), (near, 2), (other, 2)] + [(array, 0) for array in pairs]
    crosses = cross_halves(hot, lengths, sources[:2], [])
    wide = rotate_back(where, task_basis, quarters, [crosses[0][0]])
    odd = expand(1, 1, where, high, low, wide, [])
    even = expand(0, 1, where, high, low, wide, [])
    sums = sum_pairs(even, swap(odd, "narrow", 1))
    odd = expand(1, 0, where, high, low, wide, [sums[0]])
    even = expand(0, 0, where, high, low, wide, [sums[0]])
    later = sum_pairs(even, swap(odd, "narrow", 1))
    total = [sums[0]] + [swap(sums[d], "narrow", 2 * d) for d in (1, 2, 3)]
    total = sum_blocks(total, [later[0]])[0]
    mirror = swap(total, "narrow", 8)
    crosses += cross_halves(hot, lengths, sources[2:5], [total])
    total = [later[0]] + [swap(later[d], "narrow", 2 * d) for d in (1, 2, 3)]
    block, coefficients = sum_blocks(total + [mirror], [crosses[4][0]], 2)

    mirror = swap(block, "narrow", 8)
    crosses += cross_halves(hot, lengths, sources[5:], [block])
    near = stack([block] + [swap(block, "narrow", 2 * d) for d in (1, 2, 3)], [mirror, crosses[6][0]])
    other = swap(near, "narrow", 1)
    start = predict(near, other, 0, *crosses[0:2], None, 0, 2048)
    means = predict(near, other, 2, *crosses[2:4], start, 0, 2048)
    far = [mirror] + [swap(mirror, "narrow", 2 * d) for d in (1, 2, 3)]
    near = stack(far[:2], [start])
    other = swap(near, "narrow", 1)
    after = [means]
    means = predict(near, other, 0, *crosses[4:6], means, 0, 2048)
    near = stack(far[2:], after)
    other = swap(near, "narrow", 1)
    last = {g: predict(near, other, 0, *crosses[6:8], means, g * 512, 512) for g in (2, 1, 3, 0)}
    begun = sum_two(last[0], swap(last[2], "wide", 8))
    quarters = sum_quarters([begun] + [swap(last[g], "wide", 4 * g) for g in (1, 3)])
    ends = [quarters[0]] + [swap(quarters[g], "wide", g) for g in (1, 2, 3)]
    return coefficients, finish(signal, ends, task_basis, task_values[None])


def solution(mesh):
    return jax.shard_map(
        local,
        mesh=mesh,
        in_specs=(
            P("wide", "narrow"),
            P("narrow"),
            P(),
            P(),
            P(),
            P(("wide", "narrow"), None),
            P(("wide", "narrow")),
            P(),
            P(),
            P("wide"),
        ),
        out_specs=(P(("wide", "narrow"), None), P(("wide", "narrow"), None)),
        check_vma=False,
    )
```

```python
import functools
import math

import jax
import jax.numpy as jnp
from jax import lax
from jax.experimental import pallas as pl
from jax.experimental.pallas import tpu as pltpu
from jax.sharding import PartitionSpec as P

F32 = jnp.float32
BF16 = jnp.bfloat16
VM = pltpu.VMEM
MIB = 1 << 20


def far_memory(value):
    return pltpu.with_memory_space_constraint(value, pltpu.HBM)


def split(x):
    high = x.astype(BF16)
    return high, (x - high.astype(F32)).astype(BF16)


def mul(a, b, dims=(((1,), (0,)), ((), ()))):
    return lax.dot_general(a, b, dims, preferred_element_type=F32)


def mul3(a, b, dims=(((1,), (0,)), ((), ()))):
    ah, al = split(a)
    bh, bl = split(b)
    return mul(ah, bh, dims) + (mul(ah, bl, dims) + mul(al, bh, dims))


NT = (((1,), (1,)), ((), ()))


def swap(value, axis, bits):
    return lax.ppermute(value, axis, [(i, i ^ bits) for i in range(16)])


def full(shape):
    return pl.BlockSpec(shape, lambda *_: (0,) * len(shape))


def params(mib):
    return pltpu.CompilerParams(vmem_limit_bytes=mib * MIB)


def here(count):
    return [pl.BlockSpec(memory_space=VM)] * count


def scalars(count):
    return [pl.BlockSpec(memory_space=pltpu.SMEM)] * count


def anywhere(count):
    return [pl.BlockSpec(memory_space=pl.ANY)] * count


def struct(shape, dtype=F32):
    return jax.ShapeDtypeStruct(shape, dtype)


def cost(flops=0, moved=0, transcendentals=0):
    return pl.CostEstimate(flops=flops, bytes_accessed=moved, transcendentals=transcendentals)


def halves_kernel(basis, high, low, held, arrived):
    def fetch(step):
        rows = pl.ds(pl.multiple_of(step * 512, 512), 512)
        return pltpu.make_async_copy(basis.at[rows, :], held.at[rows, :], arrived.at[step])

    for step in range(8):
        fetch(step).start()

    def part(step, carry):
        fetch(step).wait()
        rows = pl.ds(pl.multiple_of(step * 512, 512), 512)
        h, l = split(held[rows, :])
        high[rows, :] = h
        low[rows, :] = l
        return carry

    lax.fori_loop(0, 8, part, 0)


def halves(basis):
    return pl.pallas_call(
        halves_kernel,
        in_specs=anywhere(1),
        out_specs=here(2),
        out_shape=[struct((4096, 512), BF16)] * 2,
        scratch_shapes=[pltpu.VMEM((4096, 512), F32), pltpu.SemaphoreType.DMA((8,))],
        compiler_params=params(20),
        cost_estimate=cost(1, 1),
        name="basis_halves",
    )(far_memory(basis))


def stack_kernel(count, *refs):
    for place in range(count):
        refs[-1][place] = refs[place][...]


def stack(values, after):
    return pl.pallas_call(
        functools.partial(stack_kernel, len(values)),
        in_specs=here(len(values)) + anywhere(len(after)),
        out_specs=here(1)[0],
        out_shape=struct((len(values), *values[0].shape)),
        compiler_params=params(3),
        name="stack",
    )(*values, *after)


def own_kernel(where, observations, codes, out):
    out[0:128, :] = observations[...].T
    out[128:136, :] = jnp.broadcast_to(codes[...].astype(F32), (8, 256))


def own_block(where, observations, codes):
    return pl.pallas_call(
        own_kernel,
        grid=(1,),
        in_specs=scalars(1) + [full((256, 128)), full((1, 256))],
        out_specs=full((136, 256)),
        out_shape=struct((136, 256)),
        compiler_params=params(2),
        name="own_observations",
    )(where, far_memory(observations), far_memory(codes[None]))


def project_part(me, high, low, total, near, other, first, far):
    def step(i, total):
        for part in range(2):
            for core, ref in enumerate((near, other)):
                slot = (first + i * 2 + part) * 2 + core + far * 8
                rows = pl.ds(pl.multiple_of((me ^ slot) * 256, 256), 256)
                oh, ol = split(ref[i * 2 + part, 0:128, :])
                both = mul(jnp.concatenate([oh, ol], axis=0), high[rows, :])
                total = total + both[:128] + (both[128:] + mul(oh, low[rows, :]))
        return total

    return lax.fori_loop(0, near.shape[0] // 2, step, total)


def near_kernel(where, high, low, near, other, out):
    out[...] = project_part(where[0], high, low, jnp.zeros((128, 512), F32), near, other, 0, 0)


def project_near(where, high, low, near, other):
    return pl.pallas_call(
        near_kernel,
        in_specs=scalars(1) + here(4),
        out_specs=here(1)[0],
        out_shape=struct((128, 512)),
        compiler_params=params(16),
        cost_estimate=cost(1, 1),
        name="project_near",
    )(where, high, low, near, other)


def project_kernel(where, high, low, task_basis, cand, before, near0, other0, near1, other1, *refs):
    outs, rotated = refs[:4], refs[4]
    me, x = where[0], where[1] // 4
    total = project_part(me, high, low, before[...], near0, other0, 0, 1)
    total = project_part(me, high, low, total, near1, other1, 2, 1)
    rotated[...] = mul3(task_basis[...].T, total)
    columns = pl.ds(pl.multiple_of(me * 128, 128), 128)
    codes = jnp.broadcast_to(cand[:, columns].astype(F32), (8, 128))
    for d in range(4):
        outs[d][0:32, :] = rotated[pl.ds(pl.multiple_of((x ^ d) * 32, 32), 32), :]
        outs[d][32:40, :] = jnp.concatenate([codes] * 4, axis=1)


def project(where, high, low, task_basis, cand, before, pairs):
    return pl.pallas_call(
        project_kernel,
        in_specs=scalars(1) + here(9),
        out_specs=here(4),
        out_shape=[struct((40, 512))] * 4,
        scratch_shapes=[pltpu.VMEM((128, 512), F32)],
        compiler_params=params(16),
        cost_estimate=cost(1, 1),
        name="project",
    )(where, high, low, task_basis, cand, before, *pairs)


def collect_kernel(own, a, b, c, out):
    out[0:32, :] = (own[0:32, :] + a[0:32, :]) + (b[0:32, :] + c[0:32, :])
    rows = [ref[32:33, :] for ref in (own, a, b, c)]
    out[32:40, :] = jnp.concatenate(rows + rows, axis=0)


def collect(pieces):
    return pl.pallas_call(
        collect_kernel,
        in_specs=here(4),
        out_specs=here(1)[0],
        out_shape=struct((40, 512)),
        compiler_params=params(2),
        name="sum_over_x",
    )(*pieces)


def scale_kernel(where, noise, conf_values, task_values, own, a, b, c, out, codes, column):
    column[...] = jnp.broadcast_to(task_values[...], (128, 128)).T
    rows = pl.ds(pl.multiple_of(where[1] // 4 * 32, 32), 32)
    total = (own[0:32, :] + a[0:32, :]) + (b[0:32, :] + c[0:32, :])
    out[...] = total / (conf_values[...] * column[rows, 0:1] + noise[0])
    for far in range(4):
        for near, ref in enumerate((own, a, b, c)):
            slot = far * 4 + near
            codes[slot : slot + 1, :] = ref[32 + far : 33 + far, 0:128]


def scale(where, noise, conf_values, task_values, pieces):
    return pl.pallas_call(
        scale_kernel,
        in_specs=scalars(2) + here(6),
        out_specs=here(2),
        out_shape=[struct((32, 512)), struct((16, 128))],
        scratch_shapes=[pltpu.VMEM((128, 128), F32)],
        compiler_params=params(2),
        name="scale",
    )(where, noise, conf_values, task_values, *pieces)


def back_kernel(where, task_basis, a, b, c, d, *refs):
    out, scaled = refs[-2:]
    x = where[1] // 4
    for far, ref in enumerate((a, b, c, d)):
        scaled[pl.ds(pl.multiple_of((x ^ far) * 32, 32), 32), :] = ref[...]
    kh, kl = split(mul3(scaled[...].T, task_basis[...], NT))
    out[:, 0:128] = kh
    out[:, 128:256] = kl


def rotate_back(where, task_basis, pieces, after):
    return pl.pallas_call(
        back_kernel,
        in_specs=scalars(1) + here(5) + anywhere(len(after)),
        out_specs=here(1)[0],
        out_shape=struct((512, 256), BF16),
        scratch_shapes=[pltpu.VMEM((128, 512), F32)],
        compiler_params=params(4),
        name="rotate_back",
    )(where, task_basis, *pieces, *after)


def expand_kernel(core, far, where, high, low, wide, *refs):
    def step(i, carry):
        for d in (i * 2, i * 2 + 1):
            slot = d * 2 + core + far * 8
            rows = pl.ds(pl.multiple_of((where[0] ^ slot) * 256, 256), 256)
            both = mul(high[rows, :], wide[...])
            refs[-1][d] = both[:, :128] + (both[:, 128:] + mul(low[rows, :], wide[:, 0:128]))
        return carry

    lax.fori_loop(0, 2, step, 0)


def expand(core, far, where, high, low, wide, after):
    return pl.pallas_call(
        functools.partial(expand_kernel, core, far),
        in_specs=scalars(1) + here(3) + anywhere(len(after)),
        out_specs=here(1)[0],
        out_shape=struct((4, 256, 128)),
        compiler_params=params(14),
        cost_estimate=cost(1, 1),
        name="expand",
    )(where, high, low, wide, *after)


def pairs_kernel(mine, theirs, *outs):
    for d in range(4):
        outs[d][...] = mine[d] + theirs[d]


def sum_pairs(mine, theirs):
    return pl.pallas_call(
        pairs_kernel,
        in_specs=here(2),
        out_specs=here(4),
        out_shape=[struct((256, 128))] * 4,
        compiler_params=params(6),
        name="sum_over_core",
    )(mine, theirs)


def sum_kernel(count, copies, *refs):
    total = refs[0][...]
    for ref in refs[1:count]:
        total = total + ref[...]
    for ref in refs[-copies:]:
        ref[...] = total


def sum_blocks(blocks, after, copies=1):
    return pl.pallas_call(
        functools.partial(sum_kernel, len(blocks), copies),
        in_specs=here(len(blocks)) + anywhere(len(after)),
        out_specs=here(copies),
        out_shape=[struct((256, 128))] * copies,
        compiler_params=params(2),
        name="sum_over_y",
    )(*blocks, *after)


def row_digit(codes, k):
    part = (k >= 40).astype(jnp.int32) + (k >= 80).astype(jnp.int32) + (k >= 120).astype(jnp.int32)
    rest = k - 40 * part
    return part, rest & 3, lax.shift_right_logical(codes, 2 * lax.shift_right_logical(rest, 2)) & 3


def onehot_kernel(length_scales, codes, out, lengths):
    k = lax.broadcasted_iota(jnp.int32, (128, 128), 0)
    part, _, _ = row_digit(k, k)
    feature = lax.shift_right_logical(k - 40 * part, 2)
    value = jnp.zeros((128, 128), F32)
    for place in range(10):
        value = jnp.where(feature == place, length_scales[place] * (-1.0 / math.log(2.0)), value)
    lengths[...] = value

    for slot in range(16):
        row = codes[slot : slot + 1, :].astype(jnp.int32)
        _, level, digit = row_digit(jnp.broadcast_to(row, (128, 128)), k)
        hot = jnp.where(digit == level, 1.0, 0.0).astype(F32)
        out[slot * 128 : slot * 128 + 128, :] = hot.T.astype(BF16)


def onehot(length_scales, codes):
    return pl.pallas_call(
        onehot_kernel,
        in_specs=scalars(1) + here(1),
        out_specs=here(2),
        out_shape=[struct((2048, 128), BF16), struct((128, 128))],
        compiler_params=params(2),
        name="candidate_levels",
    )(length_scales, codes)


def cross_kernel(firsts, hot, lengths, *refs):
    count = len(firsts)
    outs, table = refs[-1 - 2 * count : -1], refs[-1]
    k = lax.broadcasted_iota(jnp.int32, (128, 256), 0)
    length = jnp.concatenate([lengths[...], lengths[...]], axis=1)
    for place, first in enumerate(firsts):
        for part in range(2):
            row = refs[place][first + part, 128:129, :].astype(jnp.int32)
            piece, level, digit = row_digit(jnp.broadcast_to(row, (128, 256)), k)
            differ = (level - digit).astype(F32)
            value = length * differ * differ
            one = value.astype(BF16).astype(F32)
            two = (value - one).astype(BF16).astype(F32)
            three = value - one - two
            value = jnp.where(piece == 0, one, jnp.where(piece == 1, two, jnp.where(piece == 2, three, 0.0)))
            table[:, part * 256 : part * 256 + 256] = value.astype(BF16)

        def step(i, carry, high=outs[2 * place], low=outs[2 * place + 1]):
            for part in range(2):
                rows = pl.ds(pl.multiple_of(i * (256 * 2) + part * 256, 256), 256)
                h, l = split(jnp.exp2(mul(hot[rows, :], table[...])))
                high[rows, :] = h
                low[rows, :] = l
            return carry

        lax.fori_loop(0, 8 // 2, step, 0)


def cross_halves(hot, lengths, sources, after):
    arrays, firsts = zip(*sources)
    count = len(sources)
    outs = pl.pallas_call(
        functools.partial(cross_kernel, firsts),
        in_specs=here(2 + count) + anywhere(len(after)),
        out_specs=here(2 * count),
        out_shape=[struct((2048, 512), BF16)] * (2 * count),
        scratch_shapes=[pltpu.VMEM((128, 512), BF16)],
        compiler_params=params(16),
        cost_estimate=cost(1, 1),
        name="cross",
    )(hot, lengths, *arrays, *after)
    return [tuple(outs[2 * place : 2 * place + 2]) for place in range(count)]


def predict_kernel(first, near_first, has_total, near, other, h0, l0, h1, l1, *refs):
    total, out, wide = (refs[0] if has_total else None), refs[-2], refs[-1]
    for core, ref in enumerate((near, other)):
        for part in range(2):
            rows = pl.ds(core * 512 + part * 256, 256)
            wh, wl = split(ref[near_first + part])
            wide[rows, 0:128] = wh
            wide[rows, 128:256] = wl

    def step(i, carry):
        for part in range(2):
            start = i * 512 + part * 256
            rows = pl.ds(pl.multiple_of(first + start, 256), 256)
            both = mul(h0[rows, :], wide[0:512, :]) + mul(h1[rows, :], wide[512:1024, :])
            rest = mul(l0[rows, :], wide[0:512, 0:128]) + mul(l1[rows, :], wide[512:1024, 0:128])
            value = both[:, :128] + (both[:, 128:] + rest)
            out[pl.ds(pl.multiple_of(start, 256), 256), :] = value if total is None else total[rows, :] + value
        return carry

    lax.fori_loop(0, out.shape[0] // 512, step, 0)


def predict(near, other, near_first, cross0, cross1, total, first, count, after=()):
    extra = [] if total is None else [total]
    return pl.pallas_call(
        functools.partial(predict_kernel, first, near_first, total is not None),
        in_specs=here(6 + len(extra)) + anywhere(len(after)),
        out_specs=here(1)[0],
        out_shape=struct((count, 128)),
        scratch_shapes=[pltpu.VMEM((1024, 256), BF16)],
        compiler_params=params(14),
        cost_estimate=cost(1, 1),
        name="predict",
    )(near, other, *cross0, *cross1, *extra, *after)


def two_kernel(a, b, out):
    out[...] = a[...] + b[...]


def sum_two(a, b):
    return pl.pallas_call(
        two_kernel,
        in_specs=here(2),
        out_specs=here(1)[0],
        out_shape=struct(a.shape),
        compiler_params=params(3),
        name="sum_two",
    )(a, b)


def quarter_kernel(a, b, c, *outs):
    for g in range(4):
        rows = pl.ds(g * 128, 128)
        outs[g][...] = a[rows, :] + (b[rows, :] + c[rows, :])


def sum_quarters(blocks):
    return pl.pallas_call(
        quarter_kernel,
        in_specs=here(3),
        out_specs=here(4),
        out_shape=[struct((128, 128))] * 4,
        compiler_params=params(3),
        name="means_over_x",
    )(*blocks)


def finish_kernel(signal, a, b, c, d, task_basis, task_values, out):
    kernel = mul3(task_basis[...] * task_values[...], task_basis[...], NT)
    out[...] = signal[0] * mul3((a[...] + b[...]) + (c[...] + d[...]), kernel)


def finish(signal, parts, task_basis, task_values):
    return pl.pallas_call(
        finish_kernel,
        in_specs=scalars(1) + here(6),
        out_specs=here(1)[0],
        out_shape=struct((128, 128)),
        compiler_params=params(2),
        name="finish",
    )(signal, *parts, task_basis, task_values)


def local(
    basis,
    conf_values,
    task_basis,
    task_values,
    noise,
    observations,
    train_codes,
    length_scales,
    signal,
    cand_codes,
):
    n = lax.axis_index("narrow").astype(jnp.int32)
    w = lax.axis_index("wide").astype(jnp.int32)
    where = jnp.stack([n, w])

    own = own_block(where, observations, train_codes)
    high, low = halves(basis)
    mirror = swap(own, "narrow", 8)
    near = stack([own] + [swap(own, "narrow", 2 * d) for d in (1, 2, 3)], [high, mirror])
    other = swap(near, "narrow", 1)
    before = project_near(where, high, low, near, other)
    far = [mirror] + [swap(mirror, "narrow", 2 * d) for d in (1, 2, 3)]
    pairs = []
    for pair in (stack(far[:2], []), stack(far[2:], [])):
        pairs += [pair, swap(pair, "narrow", 1)]
    pieces = project(where, high, low, task_basis, cand_codes[None], before, pairs)
    mine = collect([pieces[0]] + [swap(pieces[d], "wide", 4 * d) for d in (1, 2, 3)])
    arrived = [mine] + [swap(mine, "wide", d) for d in (1, 2, 3)]
    scaled, codes = scale(where, noise, conf_values[None], task_values[None], arrived)
    quarters = [scaled] + [swap(scaled, "wide", 4 * d) for d in (1, 2, 3)]

    hot, lengths = onehot(length_scales, codes)
    sources = [(near, 0), (other, 0), (near, 2), (other, 2)] + [(array, 0) for array in pairs]
    crosses = cross_halves(hot, lengths, sources[:2], [])
    wide = rotate_back(where, task_basis, quarters, [crosses[0][0]])
    odd = expand(1, 1, where, high, low, wide, [])
    even = expand(0, 1, where, high, low, wide, [])
    sums = sum_pairs(even, swap(odd, "narrow", 1))
    odd = expand(1, 0, where, high, low, wide, [sums[0]])
    even = expand(0, 0, where, high, low, wide, [sums[0]])
    later = sum_pairs(even, swap(odd, "narrow", 1))
    total = sum_two(sums[0], swap(sums[2], "narrow", 4))
    total = [total] + [swap(sums[d], "narrow", 2 * d) for d in (1, 3)]
    total = sum_blocks(total, [later[0]])[0]
    mirror = swap(total, "narrow", 8)
    crosses += cross_halves(hot, lengths, sources[2:5], [total])
    total = sum_two(later[0], swap(later[2], "narrow", 4))
    total = [total] + [swap(later[d], "narrow", 2 * d) for d in (1, 3)]
    block, coefficients = sum_blocks(total + [mirror], [crosses[4][0]], 2)

    mirror = swap(block, "narrow", 8)
    crosses += cross_halves(hot, lengths, sources[5:], [block])
    near = stack([block] + [swap(block, "narrow", 2 * d) for d in (1, 2, 3)], [mirror, crosses[6][0]])
    other = swap(near, "narrow", 1)
    start = predict(near, other, 0, *crosses[0:2], None, 0, 2048)
    means = predict(near, other, 2, *crosses[2:4], start, 0, 2048)
    far = [mirror] + [swap(mirror, "narrow", 2 * d) for d in (1, 2, 3)]
    near = stack(far[:2], [start])
    other = swap(near, "narrow", 1)
    after = [means]
    means = predict(near, other, 0, *crosses[4:6], means, 0, 2048)
    near = stack(far[2:], after)
    other = swap(near, "narrow", 1)
    last = {g: predict(near, other, 0, *crosses[6:8], means, g * 512, 512) for g in (2, 1, 3, 0)}
    begun = sum_two(last[0], swap(last[2], "wide", 8))
    quarters = sum_quarters([begun] + [swap(last[g], "wide", 4 * g) for g in (1, 3)])
    ends = [quarters[0]] + [swap(quarters[g], "wide", g) for g in (1, 2, 3)]
    return coefficients, finish(signal, ends, task_basis, task_values[None])


def solution(mesh):
    return jax.shard_map(
        local,
        mesh=mesh,
        in_specs=(
            P("wide", "narrow"),
            P("narrow"),
            P(),
            P(),
            P(),
            P(("wide", "narrow"), None),
            P(("wide", "narrow")),
            P(),
            P(),
            P("wide"),
        ),
        out_specs=(P(("wide", "narrow"), None), P(("wide", "narrow"), None)),
        check_vma=False,
    )
```
